128 devices in a mesh: ctx: 8 (over y, x_hi), dp: 16 (over x_lo, z, core).
Axes of the slice: x: 4 (x_hi: 2, x_lo: 2; x = x_hi * 2 + x_lo), y: 4, z: 4, core: 2. Of those that a mesh axis runs over, the one named last changes fastest.
Arguments:
- events: bfloat16 [16, 4096, 512], P('dp', 'ctx'), may hold values from -6 to 6
- lengths: int32 [16, 4], P('dp'), may hold values from 1 to 3072, 4096 in all within a row
- target_rows: int32 [16, 1024], P('dp', 'ctx'), may hold values from 0 to 511, as said below
- position_ids: int32 [16, 1024], P('dp', 'ctx'), may hold values from 0 to 255
- labels: int32 [16, 1024], P('dp', 'ctx'), may hold values 0 or 1
- upstream: bfloat16 [16, 4096, 512], P('dp', 'ctx'), may hold values from -0.059814453 to 0.059814453
- w_in: bfloat16 [512, 2048], P(('ctx', 'dp')), may hold values from -0.25 to 0.25
- w_out: bfloat16 [512, 512], P(('ctx', 'dp')), may hold values from -0.25 to 0.25
- head_w1: bfloat16 [512, 256], replicated, may hold values from -0.25 to 0.25
- head_w2: float32 [256], replicated, may hold values from -0.375 to 0.375
- table: float32 [256, 128], replicated, may hold values from -6 to 6
- bias_w1: float32 [128, 128], replicated, may hold values from -0.5 to 0.5
- bias_w2: float32 [128], replicated, may hold values from -0.5 to 0.5
Outputs:
- grad_w_in: float32 [512, 2048], P(('ctx', 'dp'))
- grad_w_out: float32 [512, 512], P(('ctx', 'dp'))
- grad_head_w1: float32 [512, 256], P(('ctx', 'dp'))
- grad_head_w2: float32 [256], P(('ctx', 'dp'))
- grad_table: float32 [256, 128], P(('ctx', 'dp'))
- grad_bias_w1: float32 [128, 128], P(('ctx', 'dp'))
- grad_bias_w2: float32 [128], P(('ctx', 'dp'))
The draws below stay inside these ranges and needn't reach their ends.
Inputs may be any that keep to these rules, and one draw needn't show every extreme that they name: Each group's 4 lengths sum to 4096. `target_rows`: the 128 entries of one device are distinct.
All inputs are finite; a program needn't handle non-finite values. No bound on the sum of `labels` on one device may be relied on, other than what follows from the above.
Results may differ from the reference program's by a relative error of at most 0.0095.
Values may be sent and summed in bfloat16 or wider, within the bound.
No kernel may reach another device: no remote copies, remote signals or barrier semaphores. Data moves between devices by JAX's collectives and lax.ppermute only.
A program may use at most 192 MiB of HBM per device.

```python
import math
import jax
import jax.numpy as jnp
import numpy as np
from jax import lax

D = 512
HEADS = 4
DH = 256
DB = 128
POSITIONS = 256
LEN_DEV = 512
TGT_DEV = 128
USERS = 4
PACK = 4096
TARGETS = 1024
GROUPS = 16


def draw_target_rows(key, part):
    key = jax.random.fold_in(key, 11)
    device_keys = jax.random.split(key, GROUPS * (TARGETS // TGT_DEV))
    chosen = jax.vmap(lambda subkey: jax.random.permutation(subkey, LEN_DEV)[:TGT_DEV])(device_keys)
    return chosen.reshape(GROUPS, TARGETS).astype(jnp.int32)


def touch_ends(array, rng, low, largest):
    place = [jax.random.randint(jax.random.fold_in(rng, axis), (), 0, length) for axis, length in enumerate(array.shape)]
    widest = array.shape.index(max(array.shape))
    beside = place[:widest] + [(place[widest] + 1) % array.shape[widest]] + place[widest + 1:]
    return array.at[tuple(place)].set(low).at[tuple(beside)].set(largest)


def shard_levels(stream_key, shape, cuts, low, top_value):
    def one(dim, blocks):
        draws = jax.random.uniform(jax.random.fold_in(jax.random.fold_in(stream_key, 6), dim), (blocks,), jnp.float32, low / len(cuts), top_value / len(cuts))
        return jnp.repeat(jnp.exp(draws), shape[dim] // blocks).reshape((-1,) + (1,) * (len(shape) - dim - 1))

    level = one(*cuts[0])
    for cut in cuts[1:]:
        level = level * one(*cut)
    return level


def profile(amount, total, most, lean):
    loads = [(1 << 20) // math.isqrt(grade ** lean) + 1 for grade in range(2, amount + 1)]
    spare, given = total - most - (amount - 1), [1] * (amount - 1)
    while spare > 0:
        movable = [i for i in range(amount - 1) if given[i] < most]
        whole, remaining = sum([loads[i] for i in movable]), spare
        for i in movable:
            extra = min(most - given[i], max(1, remaining * loads[i] // whole), spare)
            given[i] = given[i] + extra
            spare = spare - extra
    return np.array([most] + given)


def uneven(own_key, amount, total, reach, skew):
    if amount == 2:
        one = jax.random.randint(own_key, (), max(1, total - reach), min(reach, total - 1) + 1)
        return jnp.stack([one, total - one])
    tallies = jnp.asarray(profile(amount, total, reach, skew), jnp.int32)
    pairs = (amount - 1) // 2
    source_of, taker = tallies[1:1 + 2 * pairs:2], tallies[2:2 + 2 * pairs:2]
    slack = jnp.minimum(source_of - 1, reach - taker)
    passed = jax.random.randint(jax.random.fold_in(own_key, 1), (pairs,), 0, 1 << 20) % (slack + 1)
    tallies = tallies.at[1:1 + 2 * pairs:2].set(source_of - passed).at[2:2 + 2 * pairs:2].set(taker + passed)
    return tallies[jax.random.permutation(jax.random.fold_in(own_key, 2), amount)]


def normal_values(own_key, extent, width, bound, cuts=(), kind=jnp.bfloat16):
    entries = jax.random.normal(own_key, extent, jnp.float32) * width
    if len(cuts) > 0:
        entries = shard_levels(own_key, extent, cuts, -0.22, 0.18) * entries
    return jnp.clip(entries, min=-bound, max=bound).astype(kind)


def setup_inputs(seed: int = 0) -> dict:
    splits = jax.random.split(jax.random.key(seed), 14)
    events = normal_values(splits[0], (GROUPS, PACK, D), 1.0, 6.0, ((0, 16), (1, 8)))
    lengths = jax.vmap(lambda own: uneven(own, USERS, PACK, 3 * PACK // USERS, 2))(jax.random.split(splits[1], GROUPS)).reshape((GROUPS, USERS)).astype(jnp.int32)
    target_rows = draw_target_rows(jax.random.fold_in(splits[13], 71), 0)
    position_ids = touch_ends(jax.random.randint(splits[3], (GROUPS, TARGETS), 0, POSITIONS), jax.random.fold_in(splits[3], 1), 0, POSITIONS - 1).astype(jnp.int32)
    labels = touch_ends((jax.random.randint(splits[4], (GROUPS, TARGETS), 0, 4) < 1).astype(jnp.int32), jax.random.fold_in(splits[4], 1), 0, 1)
    upstream = normal_values(splits[5], (GROUPS, PACK, D), 0.01, 0.059814453, ((0, 16), (1, 8)))
    w_in = normal_values(splits[6], (D, 4 * D), D ** -0.5, 0.25, ((0, 128),))
    w_out = normal_values(splits[7], (D, D), D ** -0.5, 0.25, ((0, 128),))
    head_w1 = normal_values(splits[8], (D, DH), D ** -0.5, 0.25)
    head_w2 = normal_values(splits[9], (DH,), DH ** -0.5, 0.375, (), jnp.float32)
    table = normal_values(splits[10], (POSITIONS, DB), 1.0, 6.0, (), jnp.float32)
    bias_w1 = normal_values(splits[11], (DB, DB), DB ** -0.5, 0.5, (), jnp.float32)
    bias_w2 = normal_values(splits[12], (DB,), DB ** -0.5, 0.5, (), jnp.float32)
    return {"events": events, "lengths": lengths, "target_rows": target_rows, "position_ids": position_ids, "labels": labels, "upstream": upstream, "w_in": w_in, "w_out": w_out, "head_w1": head_w1, "head_w2": head_w2, "table": table, "bias_w1": bias_w1, "bias_w2": bias_w2}


EPSILON = 1e-05
HIGHEST = lax.Precision.HIGHEST

def normalize(matrix):
    average = lax.optimization_barrier(jnp.mean(matrix, axis=-1, keepdims=True))
    centred = matrix - average
    inverse = lax.rsqrt(lax.optimization_barrier(jnp.mean(centred * centred, axis=-1, keepdims=True)) + EPSILON)
    return (centred * inverse, inverse)

def normalize_back(upward, normed, inverse):
    first = lax.optimization_barrier(jnp.mean(upward, axis=-1, keepdims=True))
    second = lax.optimization_barrier(jnp.mean(upward * normed, axis=-1, keepdims=True))
    return inverse * (upward - first - normed * second)

def silu_slope(argument):
    sigmoid_value = jax.nn.sigmoid(argument)
    return sigmoid_value * (1.0 + argument * (1.0 - sigmoid_value))

def document(positions, user_lengths):
    user_ends = jnp.cumsum(user_lengths).astype(jnp.int32)
    return lax.optimization_barrier(jnp.sum((positions[:, None] >= user_ends[None, :]).astype(jnp.int32), axis=1, dtype=jnp.int32))

def rounded(matrix):
    return lax.optimization_barrier(matrix.astype(jnp.bfloat16)).astype(jnp.float32)

def block_weights(query3, query_pos, query_doc, key3, key_pos, key_doc, score_scale):
    allowed = (query_doc[:, None] == key_doc[None, :]) & (key_pos[None, :] <= query_pos[:, None])
    scores = jnp.einsum('rhe,che->hrc', query3, key3, precision=HIGHEST) * score_scale
    weights = rounded(jnp.where(allowed[None], jax.nn.silu(scores), 0.0))
    return (allowed, scores, weights)

def block_slopes(allowed, scores, grad3, value3, score_scale):
    products = jnp.einsum('rhe,che->hrc', grad3, value3, precision=HIGHEST)
    return rounded(jnp.where(allowed[None], products * silu_slope(scores), 0.0) * score_scale)

def head_pass(picked, position_ids, labels, head_w1, head_w2, table, bias_w1, bias_w2):
    hidden = jnp.dot(picked, head_w1, preferred_element_type=jnp.float32)
    active = jax.nn.silu(hidden)
    relevance = jnp.dot(active, head_w2, precision=HIGHEST)
    slots = jnp.arange(table.shape[0], dtype=jnp.int32)
    selector = (position_ids[:, None] == slots[None, :]).astype(jnp.float32)
    embedded = jnp.dot(selector, table, precision=HIGHEST)
    bias_pre = jnp.dot(embedded, bias_w1, precision=HIGHEST)
    bias_hidden = jax.nn.silu(bias_pre)
    observe = jnp.dot(bias_hidden, bias_w2, precision=HIGHEST)
    rel_sig = jax.nn.sigmoid(relevance)
    obs_sig = jax.nn.sigmoid(observe)
    missing = jax.nn.sigmoid(-relevance) + rel_sig * jax.nn.sigmoid(-observe)
    clicked = labels.astype(jnp.float32)
    d_relevance = clicked * (rel_sig - 1.0) + (1.0 - clicked) * rel_sig * (1.0 - rel_sig) * obs_sig / missing
    d_observe = clicked * (obs_sig - 1.0) + (1.0 - clicked) * rel_sig * obs_sig * (1.0 - obs_sig) / missing
    d_hidden = (d_relevance[:, None] * head_w2[None, :] * silu_slope(hidden)).astype(jnp.bfloat16)
    grad_h1 = lax.dot_general(picked, d_hidden, (((0,), (0,)), ((), ())), preferred_element_type=jnp.float32)
    grad_h2 = jnp.dot(d_relevance, active, precision=HIGHEST)
    d_bias = d_observe[:, None] * bias_w2[None, :] * silu_slope(bias_pre)
    grad_b1 = jnp.dot(embedded.T, d_bias, precision=HIGHEST)
    grad_b2 = jnp.dot(d_observe, bias_hidden, precision=HIGHEST)
    d_embedded = jnp.dot(d_bias, bias_w1.T, precision=HIGHEST)
    grad_tab = jnp.dot(selector.T, d_embedded, precision=HIGHEST)
    d_picked = lax.dot_general(d_hidden, head_w1, (((1,), (1,)), ((), ())), preferred_element_type=jnp.float32).astype(jnp.bfloat16)
    return (grad_h1, grad_h2, grad_tab, grad_b1, grad_b2, d_picked)

def group_pass(events, user_lengths, target_rows, position_ids, labels, upstream, w_in, w_out, head_w1, head_w2, table, bias_w1, bias_w2):
    total_rows, feature_width = events.shape
    head_size = feature_width // HEADS
    score_scale = 1.0 / math.sqrt(head_size)
    normed, _ = normalize(events.astype(jnp.float32))
    normed = normed.astype(jnp.bfloat16)
    preact = jnp.dot(normed, w_in, preferred_element_type=jnp.float32)
    projected = jax.nn.silu(preact).astype(jnp.bfloat16)
    gate_rows = projected[:, :feature_width].astype(jnp.float32)
    value3 = projected[:, feature_width:2 * feature_width].astype(jnp.float32).reshape(total_rows, HEADS, head_size)
    query3 = projected[:, 2 * feature_width:3 * feature_width].astype(jnp.float32).reshape(total_rows, HEADS, head_size)
    key3 = projected[:, 3 * feature_width:].astype(jnp.float32).reshape(total_rows, HEADS, head_size)
    positions = jnp.arange(total_rows, dtype=jnp.int32)
    owners = document(positions, user_lengths)
    blocks = total_rows // LEN_DEV

    def forward_block(block_index):
        first_row = (block_index * LEN_DEV).astype(jnp.int32)
        query_block = lax.dynamic_slice_in_dim(query3, first_row, LEN_DEV, 0)
        query_pos = first_row + jnp.arange(LEN_DEV, dtype=jnp.int32)
        query_doc = lax.dynamic_slice_in_dim(owners, first_row, LEN_DEV, 0)
        _, _, weights = block_weights(query_block, query_pos, query_doc, key3, positions, owners, score_scale)
        return jnp.einsum('hrc,che->rhe', weights, value3, precision=HIGHEST).reshape(LEN_DEV, feature_width)
    attended = lax.map(forward_block, jnp.arange(blocks, dtype=jnp.int32)).reshape(total_rows, feature_width)
    attn_norm, inverse = normalize(attended)
    gated = (attn_norm * gate_rows).astype(jnp.bfloat16)
    layer_out = (jnp.dot(gated, w_out, preferred_element_type=jnp.float32) + events.astype(jnp.float32)).astype(jnp.bfloat16)
    block_of = jnp.arange(target_rows.shape[0], dtype=jnp.int32) // TGT_DEV
    where_rows = (block_of * LEN_DEV + target_rows).astype(jnp.int32)
    picked = layer_out[where_rows]
    grad_h1, grad_h2, grad_tab, grad_b1, grad_b2, d_picked = head_pass(picked, position_ids, labels, head_w1, head_w2, table, bias_w1, bias_w2)
    d_out = upstream.astype(jnp.float32).at[where_rows].add(d_picked.astype(jnp.float32)).astype(jnp.bfloat16)
    grad_wo = lax.dot_general(gated, d_out, (((0,), (0,)), ((), ())), preferred_element_type=jnp.float32)
    d_gated = lax.dot_general(d_out, w_out, (((1,), (1,)), ((), ())), preferred_element_type=jnp.float32)
    d_gate = d_gated * attn_norm
    d_attended = normalize_back(d_gated * gate_rows, attn_norm, inverse).astype(jnp.bfloat16)
    grad3 = d_attended.astype(jnp.float32).reshape(total_rows, HEADS, head_size)

    def backward_block(running, block_index):
        grad_keys, grad_values = running
        first_row = (block_index * LEN_DEV).astype(jnp.int32)
        query_block = lax.dynamic_slice_in_dim(query3, first_row, LEN_DEV, 0)
        grad_block = lax.dynamic_slice_in_dim(grad3, first_row, LEN_DEV, 0)
        query_pos = first_row + jnp.arange(LEN_DEV, dtype=jnp.int32)
        query_doc = lax.dynamic_slice_in_dim(owners, first_row, LEN_DEV, 0)
        allowed, scores, weights = block_weights(query_block, query_pos, query_doc, key3, positions, owners, score_scale)
        slopes = block_slopes(allowed, scores, grad_block, value3, score_scale)
        grad_query = jnp.einsum('hrc,che->rhe', slopes, key3, precision=HIGHEST)
        grad_keys = grad_keys + jnp.einsum('hrc,rhe->che', slopes, query_block, precision=HIGHEST)
        grad_values = grad_values + jnp.einsum('hrc,rhe->che', weights, grad_block, precision=HIGHEST)
        return ((grad_keys, grad_values), grad_query.reshape(LEN_DEV, feature_width))
    empty3 = jnp.zeros((total_rows, HEADS, head_size), jnp.float32)
    (grad_keys, grad_values), grad_query = lax.scan(backward_block, (empty3, empty3), jnp.arange(blocks, dtype=jnp.int32))
    d_projected = jnp.concatenate([d_gate, grad_values.reshape(total_rows, feature_width), grad_query.reshape(total_rows, feature_width), grad_keys.reshape(total_rows, feature_width)], axis=1)
    d_preact = (d_projected * silu_slope(preact)).astype(jnp.bfloat16)
    grad_wi = lax.dot_general(normed, d_preact, (((0,), (0,)), ((), ())), preferred_element_type=jnp.float32)
    return (grad_wi, grad_wo, grad_h1, grad_h2, grad_tab, grad_b1, grad_b2)

def reference(events, lengths, target_rows, position_ids, labels, upstream, w_in, w_out, head_w1, head_w2, table, bias_w1, bias_w2):

    def one_group(running, inputs):
        parts = group_pass(inputs[0], inputs[1], inputs[2], inputs[3], inputs[4], inputs[5], w_in, w_out, head_w1, head_w2, table, bias_w1, bias_w2)
        return (tuple((old + new for old, new in zip(running, parts))), None)
    start_sums = (jnp.zeros(w_in.shape, jnp.float32), jnp.zeros(w_out.shape, jnp.float32), jnp.zeros(head_w1.shape, jnp.float32), jnp.zeros(head_w2.shape, jnp.float32), jnp.zeros(table.shape, jnp.float32), jnp.zeros(bias_w1.shape, jnp.float32), jnp.zeros(bias_w2.shape, jnp.float32))
    sums, _ = lax.scan(one_group, start_sums, (events, lengths, target_rows, position_ids, labels, upstream))
    return (sums[0], sums[1], sums[2], sums[3], sums[4], sums[5], sums[6])
```

```python
import functools
import math

import jax
import jax.numpy as jnp
from jax import lax
from jax.experimental import pallas as pl
from jax.experimental.pallas import tpu as pltpu
from jax.sharding import Mesh, PartitionSpec as P

HEADS = 4
EPSILON = 1e-05
HIGHEST = lax.Precision.HIGHEST
F32 = jnp.float32
BF16 = jnp.bfloat16
I32 = jnp.int32
R = 512
W = 512
E = 128
T = 128
SCALE = 1.0 / math.sqrt(E)
HALF = 0.5 * SCALE

NN = (((1,), (0,)), ((), ()))
NT = (((1,), (1,)), ((), ()))
TN = (((0,), (0,)), ((), ()))


def mm(a, b, dims=NN, precision=None):
    return lax.dot_general(a, b, dims, precision=precision, preferred_element_type=F32)


def silu_parts(z):
    h = 0.5 * z
    t = jnp.tanh(h)
    a = 1.0 + t
    w = h * a
    return w, 0.5 * (a + w * (1.0 - t))


def silu(z):
    h = 0.5 * z
    return h + h * jnp.tanh(h)


def vmem(n):
    return [pl.BlockSpec(memory_space=pltpu.VMEM)] * n


def smem():
    return [pl.BlockSpec(memory_space=pltpu.SMEM)]


def call(kernel, outs, args, scratch=(), limit=40, flops=0, n_smem=1, name=None):
    total = sum(a.size * a.dtype.itemsize for a in args) + sum(
        math.prod(o.shape) * o.dtype.itemsize for o in outs
    )
    return pl.pallas_call(
        kernel,
        out_shape=tuple(outs),
        in_specs=smem() * n_smem + vmem(len(args) - n_smem),
        out_specs=tuple(vmem(len(outs))),
        scratch_shapes=list(scratch),
        compiler_params=pltpu.CompilerParams(vmem_limit_bytes=limit << 20),
        cost_estimate=pl.CostEstimate(flops=flops, bytes_accessed=total, transcendentals=0),
        name=name,
    )(*args)


def sds(shape, dtype):
    return jax.ShapeDtypeStruct(shape, dtype)


def norm_kernel(x_ref, o_ref):
    x = x_ref[...].astype(F32)
    mean = jnp.mean(x, axis=-1, keepdims=True)
    cen = x - mean
    inv = lax.rsqrt(jnp.mean(cen * cen, axis=-1, keepdims=True) + EPSILON)
    o_ref[...] = (cen * inv).astype(BF16)


def user_start(pos, meta):
    start = jnp.zeros_like(pos)
    end = 0
    for j in range(3):
        end = end + meta[2 + j]
        start = jnp.where(pos >= end, end, start)
    return start


def forward_kernel(meta, n0, n1, n3, n2a, n2b, o0, o1, o3, o2a, o2b, wg, a0, a1, a2, a3, q_s, k_s, v_s):
    y, core = meta[0], meta[1]
    own = ((0, (n0,)), (1, (n1,)), (3, (n3,)), (2, (n2a, n2b)))
    oth = ((0, (o0,)), (1, (o1,)), (3, (o3,)), (2, (o2a, o2b)))
    for k, refs in own:
        blk = (y + 4 - k) & 3
        b = 2 * blk + core
        at = 0
        for ref in refs:
            n = ref.shape[0]
            p = silu(mm(ref[...], wg[:, : 3 * E])).astype(BF16)
            q_s[blk, at : at + n] = p[:, :E]
            k_s[b, at : at + n] = p[:, E : 2 * E]
            v_s[b, at : at + n] = p[:, 2 * E :]
            at += n
    for k, refs in oth:
        b = 2 * ((y + 4 - k) & 3) + 1 - core
        at = 0
        for ref in refs:
            n = ref.shape[0]
            p = silu(mm(ref[...], wg[:, E : 3 * E])).astype(BF16)
            k_s[b, at : at + n] = p[:, :E]
            v_s[b, at : at + n] = p[:, E:]
            at += n
    rows = lax.broadcasted_iota(I32, (R, 1), 0)
    lanes = lax.broadcasted_iota(I32, (1, R), 1)
    for k, out in enumerate((a0, a1, a2, a3)):
        blk = (y + k) & 3
        c = 2 * blk + core
        q = q_s[blk]
        pos = rows + c * R
        start = user_start(pos, meta)

        def step(b, acc):
            key_pos = lanes + b * R
            h = mm(q, k_s[b], NT) * HALF
            w = h + h * jnp.tanh(h)
            w = jnp.where((key_pos >= start) & (key_pos <= pos), w, 0.0).astype(BF16)
            return acc + mm(w, v_s[b])

        lo = user_start(c * R, meta) // R
        out[...] = lax.fori_loop(lo, c + 1, step, jnp.zeros((R, E), F32)).astype(BF16)


def side_kernel(
    meta, n0, n1, n3, n2a, n2b, o0, o1, o3, o2a, o2b, wg, wo_half, events, ints, table, bias_w1, bias_w2,
    sq, sk, sv, nt, u, su, w_out, ev_t, emb, bpre, obs,
):
    y, core = meta[0], meta[1]
    own = ((0, (n0,)), (1, (n1,)), (3, (n3,)), (2, (n2a, n2b)))
    oth = ((0, (o0,)), (1, (o1,)), (3, (o3,)), (2, (o2a, o2b)))
    for k, refs in own:
        blk = (y + 4 - k) & 3
        b = 2 * blk + core
        at = 0
        for ref in refs:
            n = ref.shape[0]
            x = ref[...]
            _, s = silu_parts(mm(x, wg[:, : 3 * E]))
            s = s.astype(BF16)
            sq[blk, at : at + n] = s[:, :E]
            sk[b, at : at + n] = s[:, E : 2 * E]
            sv[b, at : at + n] = s[:, 2 * E :]
            nt[b, :, at : at + n] = x.T
            at += n
    for k, refs in oth:
        b = 2 * ((y + 4 - k) & 3) + 1 - core
        at = 0
        for ref in refs:
            n = ref.shape[0]
            x = ref[...]
            _, s = silu_parts(mm(x, wg[:, E : 3 * E]))
            s = s.astype(BF16)
            sk[b, at : at + n] = s[:, :E]
            sv[b, at : at + n] = s[:, E:]
            nt[b, :, at : at + n] = x.T
            at += n
    first = core == 0
    mine = wg[:, 3 * E :]
    other = wo_half[...]
    w_u = jnp.where(first, mine, other)
    w_out[...] = jnp.where(first, other, mine)
    act, slope = silu_parts(mm(n0[...], w_u))
    u[...] = act.astype(BF16)
    su[...] = slope.astype(BF16)
    placing = (lax.broadcasted_iota(I32, (R, T), 0) == ints[0:1, :]).astype(BF16)
    ev_t[...] = mm(placing, events[...], TN)
    pid = jnp.broadcast_to(ints[1:2, :], (T, T)).astype(F32).T.astype(I32)
    pid = jnp.concatenate([pid, pid], axis=1)
    selector = (lax.broadcasted_iota(I32, (T, 2 * T), 1) == pid).astype(F32)
    embedded = mm(selector, table[...], precision=HIGHEST)
    bias_pre = mm(embedded, bias_w1[...], precision=HIGHEST)
    emb[...] = embedded
    bpre[...] = bias_pre
    hid, _ = silu_parts(bias_pre)
    obs[...] = jnp.broadcast_to(jnp.sum(hid * bias_w2[...], axis=1, keepdims=True), (T, E))


def middle_kernel(
    meta, r0, r1, r2, r3, u, su, w_out, ev_t, obs, ints, upstream, head_w1, head_w2,
    d0, d1, d2, d3, gated_o, dout_o, dpre_o, picked_o, dhid_o, act_o, drel_o, dobs_o,
    att,
):
    y = meta[0]
    for k, ref in enumerate((r0, r1, r2, r3)):
        h = (y + 4 - k) & 3
        att[:, pl.ds(pl.multiple_of(h * E, E), E)] = ref[...].astype(F32)
    x = att[...]
    mean = jnp.mean(x, axis=-1, keepdims=True)
    cen = x - mean
    inv = lax.rsqrt(jnp.mean(cen * cen, axis=-1, keepdims=True) + EPSILON)
    normed = cen * inv
    gate = u[...].astype(F32)
    gated = (normed * gate).astype(BF16)
    gated_o[...] = gated
    placing = (lax.broadcasted_iota(I32, (R, T), 0) == ints[0:1, :]).astype(BF16)
    gated_t = mm(placing, gated, TN).astype(BF16)
    picked = (mm(gated_t, w_out[...]) + ev_t[...]).astype(BF16)
    picked_o[...] = picked
    hidden = mm(picked, head_w1[...])
    active, slope = silu_parts(hidden)
    act_o[...] = active
    w2 = head_w2[...]
    relevance = jnp.sum(active * w2, axis=1, keepdims=True)
    observe = obs[:, :1]
    clicked = jnp.broadcast_to(ints[2:3, :], (T, T)).astype(F32).T[:, :1]
    rel_sig = jax.nn.sigmoid(relevance)
    obs_sig = jax.nn.sigmoid(observe)
    missing = jax.nn.sigmoid(-relevance) + rel_sig * jax.nn.sigmoid(-observe)
    d_rel = clicked * (rel_sig - 1.0) + (1.0 - clicked) * rel_sig * (1.0 - rel_sig) * obs_sig / missing
    d_obs = clicked * (obs_sig - 1.0) + (1.0 - clicked) * rel_sig * obs_sig * (1.0 - obs_sig) / missing
    drel_o[...] = jnp.broadcast_to(d_rel, (T, E))
    dobs_o[...] = jnp.broadcast_to(d_obs, (T, E))
    d_hidden = (d_rel * w2 * slope).astype(BF16)
    dhid_o[...] = d_hidden
    d_picked = mm(d_hidden, head_w1[...], NT).astype(BF16)
    d_out = (upstream[...].astype(F32) + mm(placing, d_picked)).astype(BF16)
    dout_o[...] = d_out
    d_gated = mm(d_out, w_out[...], NT)
    dpre_o[...] = (d_gated * normed * su[...].astype(F32)).astype(BF16)
    g = d_gated * gate
    first = jnp.mean(g, axis=-1, keepdims=True)
    second = jnp.mean(g * normed, axis=-1, keepdims=True)
    att[...] = inv * (g - first - normed * second)
    for k, ref in enumerate((d0, d1, d2, d3)):
        h = (y + k) & 3
        ref[...] = att[:, pl.ds(pl.multiple_of(h * E, E), E)].astype(BF16)


def packed(left, right):
    low = (lax.broadcasted_iota(I32, left.shape, 0) & 7) < 4
    n = left.shape[0]
    return jnp.where(low, left, pltpu.roll(right, 4, 0)), jnp.where(low, pltpu.roll(left, n - 4, 0), right)


def grads_kernel(
    meta, nt_own, dpre, gated, d_out, picked, d_hid, active, d_rel, d_obs, ints, emb, bpre, bias_w1, bias_w2,
    x_own, x_oth, s_own, s_oth,
):
    first = meta[1] == 0

    def put(own_ref, oth_ref, col, left, right):
        x_0, x_1 = packed(left, right)
        cols = slice(col, col + left.shape[1])
        own_ref[:, cols] = jnp.where(first, x_0, x_1).astype(BF16)
        oth_ref[:, cols] = jnp.where(first, x_1, x_0).astype(BF16)

    g_u = mm(nt_own[0], dpre[...])
    put(x_own, x_oth, 0, g_u[:, :256], g_u[:, 256:])
    g_wo = mm(gated[...], d_out[...], TN)
    put(x_own, x_oth, 256, g_wo[:, :256], g_wo[:, 256:])
    g_h1 = mm(picked[...], d_hid[...], TN)
    put(x_own, x_oth, 512, g_h1[:, :128], g_h1[:, 128:])
    hid, slope = silu_parts(bpre[...])
    d_bias = d_obs[...] * bias_w2[...] * slope
    g_b1 = mm(emb[...], d_bias, TN, HIGHEST)
    d_emb = mm(d_bias, bias_w1[...], NT, HIGHEST)
    pid = jnp.broadcast_to(ints[1:2, :], (2 * T, T))
    select_t = (lax.broadcasted_iota(I32, (2 * T, T), 0) == pid).astype(F32)
    g_tab = mm(select_t, d_emb, precision=HIGHEST)
    h2 = mm(active[...], d_rel[...], TN, HIGHEST)
    b2 = mm(hid, d_obs[...], TN, HIGHEST)
    lane2 = lax.broadcasted_iota(I32, (2 * T, E), 1)
    row2 = lax.broadcasted_iota(I32, (2 * T, E), 0)
    h2 = jnp.where(lane2 == (row2 & 1), h2, 0.0)
    b2 = jnp.where(lax.broadcasted_iota(I32, (T, E), 1) == 2, b2, 0.0)
    o2 = lax.broadcasted_iota(I32, (R, 2 * T), 0)
    i2 = lax.broadcasted_iota(I32, (R, 2 * T), 1)
    o1 = lax.broadcasted_iota(I32, (R, T), 0)
    i1 = lax.broadcasted_iota(I32, (R, T), 1)
    parts = []
    for cc in range(2):
        dest2 = 2 * (o2 >> 3) + cc
        dest1 = 2 * (o1 >> 3) + cc
        p_tab = (((o2 & 7) == 4) & (i2 == 2 * dest2)) | (((o2 & 7) == 5) & (i2 == 2 * dest2 + 1))
        p_h2 = ((o2 & 7) == 7) & ((i2 >> 1) == dest2)
        p_b1 = ((o1 & 7) == 6) & (i1 == dest1)
        p_b2 = ((o1 & 7) == 7) & (i1 == dest1)
        parts.append(
            mm(p_tab.astype(BF16), g_tab.astype(BF16))
            + mm(p_h2.astype(BF16), h2.astype(BF16))
            + mm(p_b1.astype(BF16), g_b1.astype(BF16))
            + mm(p_b2.astype(BF16), b2.astype(BF16))
        )
    s_own[...] = jnp.where(first, parts[0], parts[1]).astype(BF16)
    s_oth[...] = jnp.where(first, parts[1], parts[0]).astype(BF16)


def backward_kernel(
    meta, q_s, k_s, v_s, r0, r1, r2, r3, sq, sk, sv, nt, s_own, s_oth,
    x_own, x_oth,
    dq_s, dk_s, dv_s,
):
    y, core = meta[0], meta[1]
    dk_s[...] = jnp.zeros_like(dk_s)
    dv_s[...] = jnp.zeros_like(dv_s)
    rows = lax.broadcasted_iota(I32, (R, 1), 0)
    lanes = lax.broadcasted_iota(I32, (1, R), 1)
    for k, ref in enumerate((r0, r1, r2, r3)):
        blk = (y + 4 - k) & 3
        c = 2 * blk + core
        q = q_s[blk]
        g = ref[...]
        pos = lanes + c * R
        start = user_start(pos, meta)

        def step(b, dq):
            key_pos = rows + b * R
            kb = k_s[b]
            h = mm(kb, q, NT) * HALF
            dp = mm(v_s[b], g, NT)
            t = jnp.tanh(h)
            a = 1.0 + t
            w = h * a
            d = dp * (a + w * (1.0 - t))
            keep = (key_pos >= start) & (key_pos <= pos)
            w = jnp.where(keep, w, 0.0).astype(BF16)
            d = jnp.where(keep, d, 0.0).astype(BF16)
            dv_s[b] += mm(w, g)
            dk_s[b] += mm(d, q)
            return dq + mm(d, kb, TN)

        lo = user_start(c * R, meta) // R
        dq_s[blk] = lax.fori_loop(lo, c + 1, step, jnp.zeros((R, E), F32))
    g_q = jnp.zeros((W, E), F32)
    g_k = jnp.zeros((W, E), F32)
    g_v = jnp.zeros((W, E), F32)
    for i in range(4):
        b = 2 * i + core
        d = (dq_s[i] * HALF * sq[i].astype(F32)).astype(BF16)
        g_q = g_q + mm(nt[b], d)
    for b in range(8):
        d = (dk_s[b] * HALF * sk[b].astype(F32)).astype(BF16)
        g_k = g_k + mm(nt[b], d)
        d = (dv_s[b] * sv[b].astype(F32)).astype(BF16)
        g_v = g_v + mm(nt[b], d)
    first = core == 0
    low = (lax.broadcasted_iota(I32, (W, E), 0) & 7) < 4
    x_0, x_1 = packed(g_q, g_k)
    x_own[:, :E] = jnp.where(first, x_0, x_1).astype(BF16)
    x_oth[:, :E] = jnp.where(first, x_1, x_0).astype(BF16)
    v_1 = pltpu.roll(g_v, W - 4, 0)
    x_own[:, E:] = jnp.where(low, jnp.where(first, g_v, v_1), s_own[...].astype(F32)).astype(BF16)
    x_oth[:, E:] = jnp.where(low, jnp.where(first, v_1, g_v), s_oth[...].astype(F32)).astype(BF16)


def sum_kernel(x_ref, g_in, g_out, g_h1, g_small):
    total = None
    for h in range(HEADS):
        part = jnp.zeros((8, 7 * E), F32)
        for i in range(16):
            at = (h * 16 + i) * 8
            part = part + x_ref[at : at + 8, :].astype(F32)
        g_in[:, W + h * E : W + (h + 1) * E] = part[0:4, 6 * E :]
        g_in[:, 2 * W + h * E : 2 * W + (h + 1) * E] = part[0:4, 5 * E : 6 * E]
        g_in[:, 3 * W + h * E : 3 * W + (h + 1) * E] = part[4:8, 5 * E : 6 * E]
        total = part if total is None else total + part
    g_in[:, 0:256] = total[0:4, 0:256]
    g_in[:, 256:512] = total[4:8, 0:256]
    g_out[:, 0:256] = total[0:4, 256:512]
    g_out[:, 256:512] = total[4:8, 256:512]
    g_h1[:, 0:128] = total[0:4, 512:640]
    g_h1[:, 128:256] = total[4:8, 512:640]
    g_small[...] = total[4:8, 768:896]


CHIPS = ("y", "xh", "xl", "z")
SWAP = []
for _i in range(32):
    _xh, _rest, _core = _i // 16, (_i // 2) % 8, _i % 2
    SWAP.append((_i, _i if _xh == _core else (1 - _xh) * 16 + _rest * 2 + 1 - _core))


def swapped(x):
    return lax.ppermute(x, ("xh", "xl", "z", "core"), SWAP)


def across(x):
    return lax.ppermute(x, "core", [(0, 1), (1, 0)])


def ring(x, k):
    return lax.ppermute(x, "y", [(i, (i + k) % 4) for i in range(4)])


def body(
    events, lengths, target_rows, position_ids, labels, upstream,
    w_in, w_out, head_w1, head_w2, table, bias_w1, bias_w2,
):
    y, core = lax.axis_index("y"), lax.axis_index("core")
    w_rows = jnp.concatenate([w_in, w_out], axis=1)
    w_other = across(w_rows)
    w_rows = jnp.where(
        core == 0, jnp.concatenate([w_rows, w_other], axis=0), jnp.concatenate([w_other, w_rows], axis=0)
    )
    shared = jnp.where(core == 0, w_rows[:, :W], w_rows[:, 4 * W :])
    sent = jnp.stack(
        [
            jnp.concatenate(
                [
                    w_rows[:, 2 * W + h * E : 2 * W + (h + 1) * E],
                    w_rows[:, 3 * W + h * E : 3 * W + (h + 1) * E],
                    w_rows[:, W + h * E : W + (h + 1) * E],
                    shared,
                ],
                axis=1,
            )
            for h in range(HEADS)
        ]
    )
    sent = jnp.broadcast_to(sent[:, None], (4, 16, 8, 7 * E)).reshape(W, 7 * E)
    wg = lax.all_to_all(sent, CHIPS, 0, 0, tiled=True)
    w_half = across(wg[:, 3 * E :])

    ev = swapped(events[0])
    ints = swapped(
        jnp.concatenate([target_rows, position_ids, labels, jnp.pad(lengths, ((0, 0), (0, T - 4)))], axis=0)
    )
    meta = jnp.concatenate([jnp.stack([y, core]).astype(I32), ints[3, :6]])
    (n0,) = call(norm_kernel, [sds((R, W), BF16)], [ev], n_smem=0, name="norm")
    n1 = ring(n0, 1)
    n3 = ring(n0, 3)
    n2a = ring(n1[: R // 2], 1)
    n2b = ring(n3[R // 2 :], 3)
    parts = [n0, n1, n3, n2a, n2b]
    parts = parts + [across(p) for p in parts]
    up = swapped(upstream[0])

    qkv = [sds((4, R, E), BF16), sds((8, R, E), BF16), sds((8, R, E), BF16)]
    a0, a1, a2, a3, q_s, k_s, v_s = call(
        forward_kernel, [sds((R, E), BF16)] * 4 + qkv, [meta] + parts + [wg], flops=5 * 10**9, name="forward"
    )
    r1, r2, r3 = ring(a1, 1), ring(a2, 2), ring(a3, 3)
    sq, sk, sv, nt, u, su, w_o, ev_t, emb, bpre, obs = call(
        side_kernel,
        qkv
        + [sds((8, W, R), BF16)]
        + [sds((R, W), BF16)] * 3
        + [sds((T, W), F32)]
        + [sds((T, E), F32)] * 3,
        [meta] + parts + [wg, w_half, ev, ints, table, bias_w1, bias_w2.reshape(1, E)],
        flops=2 * 10**9,
        limit=48,
        name="side",
    )
    w2 = head_w2.reshape(1, 2 * E)
    b2 = bias_w2.reshape(1, E)
    d0, d1, d2, d3, gated, d_out, dpre, picked, d_hid, active, d_rel, d_obs = call(
        middle_kernel,
        [sds((R, E), BF16)] * 4
        + [sds((R, W), BF16)] * 3
        + [sds((T, W), BF16), sds((T, 2 * E), BF16), sds((T, 2 * E), F32), sds((T, E), F32), sds((T, E), F32)],
        [meta, a0, r1, r2, r3, u, su, w_o, ev_t, obs, ints, up, head_w1, w2],
        scratch=[pltpu.VMEM((R, W), F32)],
        flops=10**9,
        name="middle",
    )
    g1, g2, g3 = ring(d1, 1), ring(d2, 2), ring(d3, 3)
    nt_own = lax.dynamic_slice_in_dim(nt, 2 * y + core, 1, 0)
    early, early_oth, s_own, s_oth = call(
        grads_kernel,
        [sds((R, 5 * E), BF16)] * 2 + [sds((R, E), BF16)] * 2,
        [meta, nt_own, dpre, gated, d_out, picked, d_hid, active, d_rel, d_obs, ints, emb, bpre, bias_w1, b2],
        flops=2 * 10**9,
        name="grads",
    )
    early_in = across(early_oth)
    late, late_oth = call(
        backward_kernel,
        [sds((R, 2 * E), BF16)] * 2,
        [meta, q_s, k_s, v_s, d0, g1, g2, g3, sq, sk, sv, nt, s_own, s_oth],
        scratch=[pltpu.VMEM((4, R, E), F32), pltpu.VMEM((8, R, E), F32), pltpu.VMEM((8, R, E), F32)],
        flops=10**10,
        limit=48,
        name="backward",
    )
    late_in = across(late_oth)
    pair = jnp.concatenate(
        [
            (early.astype(F32) + early_in.astype(F32)).astype(BF16),
            (late.astype(F32) + late_in.astype(F32)).astype(BF16),
        ],
        axis=1,
    )
    got = lax.all_to_all(pair, CHIPS, 0, 0, tiled=True)
    g_in, g_out, g_h1, g_small = call(
        sum_kernel,
        [sds((4, 4 * W), F32), sds((4, W), F32), sds((4, 2 * E), F32), sds((4, E), F32)],
        [got],
        n_smem=0,
        name="total",
    )
    return g_in, g_out, g_h1, g_small[3, 0:2], g_small[0:2], g_small[2:3], g_small[3, 2:3]


def solution(mesh):
    fine = Mesh(mesh.devices.reshape(4, 2, 2, 4, 2), ("y", "xh", "xl", "z", "core"))
    ctx, dp = ("y", "xh"), ("xl", "z", "core")
    every = ctx + dp
    in_specs = (
        P(dp, ctx, None),
        P(dp, None),
        P(dp, ctx),
        P(dp, ctx),
        P(dp, ctx),
        P(dp, ctx, None),
        P(every, None),
        P(every, None),
        P(),
        P(),
        P(),
        P(),
        P(),
    )
    out_specs = (
        P(every, None),
        P(every, None),
        P(every, None),
        P(every),
        P(every, None),
        P(every, None),
        P(every),
    )
    return jax.shard_map(body, mesh=fine, in_specs=in_specs, out_specs=out_specs, check_vma=False)
```

```python
import functools
import math

import jax
import jax.numpy as jnp
from jax import lax
from jax.experimental import pallas as pl
from jax.experimental.pallas import tpu as pltpu
from jax.sharding import Mesh, PartitionSpec as P

HEADS = 4
EPSILON = 1e-05
HIGHEST = lax.Precision.HIGHEST
F32 = jnp.float32
BF16 = jnp.bfloat16
I32 = jnp.int32
R = 512
W = 512
E = 128
T = 128
SCALE = 1.0 / math.sqrt(E)
HALF = 0.5 * SCALE

NN = (((1,), (0,)), ((), ()))
NT = (((1,), (1,)), ((), ()))
TN = (((0,), (0,)), ((), ()))


def mm(a, b, dims=NN, precision=None):
    return lax.dot_general(a, b, dims, precision=precision, preferred_element_type=F32)


def silu_parts(z):
    h = 0.5 * z
    t = jnp.tanh(h)
    a = 1.0 + t
    w = h * a
    return w, 0.5 * (a + w * (1.0 - t))


def silu(z):
    h = 0.5 * z
    return h + h * jnp.tanh(h)


def vmem(n):
    return [pl.BlockSpec(memory_space=pltpu.VMEM)] * n


def smem():
    return [pl.BlockSpec(memory_space=pltpu.SMEM)]


def call(kernel, outs, args, scratch=(), limit=24, flops=0, n_smem=1, n_any=0, name=None):
    total = sum(a.size * a.dtype.itemsize for a in args) + sum(
        math.prod(o.shape) * o.dtype.itemsize for o in outs
    )
    return pl.pallas_call(
        kernel,
        out_shape=tuple(outs),
        in_specs=smem() * n_smem
        + vmem(len(args) - n_smem - n_any)
        + [pl.BlockSpec(memory_space=pl.ANY)] * n_any,
        out_specs=tuple(vmem(len(outs))),
        scratch_shapes=list(scratch),
        compiler_params=pltpu.CompilerParams(vmem_limit_bytes=limit << 20),
        cost_estimate=pl.CostEstimate(flops=flops, bytes_accessed=total, transcendentals=0),
        name=name,
    )(*args)


def sds(shape, dtype):
    return jax.ShapeDtypeStruct(shape, dtype)


def plane_kernel(coords, q0, q1, q2, q3, out):
    for k, ref in enumerate((q0, q1, q2, q3)):
        out[pl.ds(pl.multiple_of(((coords[1] + 4 - k) & 3) * 32, 32), 32), :] = ref[...]


def cube_kernel(coords, q0, q1, q2, q3, out, rows):
    for k, ref in enumerate((q0, q1, q2, q3)):
        z = ((coords[2] + 4 - k) & 3) * 8
        part = ref[...].astype(F32)
        for i in range(4):
            for j in range(4):
                at = i * 32 + j * 8
                rows[pl.ds(pl.multiple_of(j * E + i * 32 + z, 8), 8), :] = part[at : at + 8]
    out[...] = rows[...].astype(BF16)


def norm_kernel(x_ref, _, o_ref):
    x = x_ref[...].astype(F32)
    mean = jnp.mean(x, axis=-1, keepdims=True)
    cen = x - mean
    inv = lax.rsqrt(jnp.mean(cen * cen, axis=-1, keepdims=True) + EPSILON)
    o_ref[...] = (cen * inv).astype(BF16)


def user_start(pos, meta):
    start = jnp.zeros_like(pos)
    end = 0
    for j in range(3):
        end = end + meta[3, 2 + j]
        start = jnp.where(pos >= end, end, start)
    return start


def places(y, core):
    s = jnp.where(core == 0, 3, 1)
    back, on, far = (y + s) & 3, (y + 4 - s) & 3, (y + 2) & 3
    return (y, back, on, far), (y, on, back, far)


def key_range(base, rows, meta):
    lo = user_start(base, meta)
    last = base + rows - 1
    end = last // R + 1
    first = lo // R
    diag = base // R
    full = jnp.clip((user_start(last, meta) + R - 1) // R, first, diag)
    return first, full, diag, end


def forward_kernel(meta, n0, na, nb, nc, o0, oa, ob, oc, wg, a0, a1, a2, a3, q_s, k_s, v_s):
    y, core = meta[3, 0], meta[3, 1]
    own, oth = places(y, core)
    for blk, ref in zip(own, (n0, na, nb, nc)):
        b = 2 * blk + core
        p = silu(mm(ref[...], wg[:, : 3 * E])).astype(BF16)
        q_s[blk] = p[:, :E]
        k_s[b] = p[:, E : 2 * E]
        v_s[b] = p[:, 2 * E :]
    for blk, ref in zip(oth, (o0, oa, ob, oc)):
        b = 2 * blk + 1 - core
        p = silu(mm(ref[...], wg[:, E : 3 * E])).astype(BF16)
        k_s[b] = p[:, :E]
        v_s[b] = p[:, E:]
    rows = lax.broadcasted_iota(I32, (R, 1), 0)
    lanes = lax.broadcasted_iota(I32, (1, R), 1)
    for k, out in enumerate((a0, a1, a2, a3)):
        blk = (y + k) & 3
        c = 2 * blk + core
        q = q_s[blk]
        pos = rows + c * R
        start = user_start(pos, meta)

        def step(b, acc, masked):
            h = mm(q, k_s[b], NT) * HALF
            w = h + h * jnp.tanh(h)
            if masked:
                key_pos = lanes + b * R
                w = jnp.where((key_pos >= start) & (key_pos <= pos), w, 0.0)
            return acc + mm(w.astype(BF16), v_s[b])

        first, full, diag, end = key_range(c * R, R, meta)
        acc = jnp.zeros((R, E), F32)
        acc = lax.fori_loop(first, full, functools.partial(step, masked=True), acc)
        acc = lax.fori_loop(full, diag, functools.partial(step, masked=False), acc)
        acc = lax.fori_loop(diag, end, functools.partial(step, masked=True), acc)
        mean = jnp.mean(acc, axis=-1, keepdims=True).astype(BF16)
        out[:R] = (acc - mean.astype(F32)).astype(BF16)
        one = (lax.broadcasted_iota(I32, (16, E), 1) == 0).astype(BF16)
        line = mm(one, jnp.broadcast_to(mean, (R, E)), NT)
        out[R:] = jnp.concatenate(
            [line[0:1, i * E : (i + 1) * E] for i in range(4)] + [jnp.zeros((12, E), F32)], axis=0
        ).astype(BF16)


def side_kernel(
    meta, n0, wg, wo_half, events, ints, table, bias_w1, bias_w2, u, su, w_out, ev_t, emb, bpre, obs
):
    first = meta[3, 1] == 0
    mine = wg[:, 3 * E :]
    other = wo_half[...]
    w_u = jnp.where(first, mine, other)
    w_out[...] = jnp.where(first, other, mine)
    act, slope = silu_parts(mm(n0[...], w_u))
    u[...] = act.astype(BF16)
    su[...] = slope.astype(BF16)
    placing = (lax.broadcasted_iota(I32, (R, T), 0) == ints[0:1, :]).astype(BF16)
    ev_t[...] = mm(placing, events[...], TN)
    pid = jnp.broadcast_to(ints[1:2, :], (T, T)).astype(F32).T.astype(I32)
    pid = jnp.concatenate([pid, pid], axis=1)
    selector = (lax.broadcasted_iota(I32, (T, 2 * T), 1) == pid).astype(F32)
    embedded = mm(selector, table[...], precision=HIGHEST)
    bias_pre = mm(embedded, bias_w1[...], precision=HIGHEST)
    emb[...] = embedded
    bpre[...] = bias_pre
    hid = silu(bias_pre)
    obs[...] = jnp.broadcast_to(jnp.sum(hid * bias_w2[...], axis=1, keepdims=True), (T, E))


def slopes_kernel(meta, n0, na, nb, nc, wg, _, s_o, nt):
    y, core = meta[3, 0], meta[3, 1]
    width = s_o.shape[2]
    own, oth = places(y, core)
    for blk, ref in zip(own if width == 3 * E else oth, (n0, na, nb, nc)):
        x = ref[...]
        s_o[blk] = silu_parts(mm(x, wg[:, 3 * E - width : 3 * E]))[1].astype(BF16)
        nt[blk] = x.T


def middle_kernel(
    meta, r0, r1, r2, r3, u, su, w_out, ev_t, obs, ints, upstream, head_w1, head_w2,
    d0, d1, d2, d3, gated_o, dout_o, dpre_o, picked_o, dhid_o, act_o, drel_o, dobs_o,
    att,
):
    y = meta[3, 0]
    for k, ref in enumerate((r0, r1, r2, r3)):
        h = (y + 4 - k) & 3
        means = ref[R:]
        pick = lax.broadcasted_iota(I32, (16, E), 0)
        column = jnp.concatenate([mm(means, (pick == i).astype(BF16), TN) for i in range(4)], axis=0)
        att[:, pl.ds(pl.multiple_of(h * E, E), E)] = ref[:R].astype(F32) + column
    x = att[...]
    mean = jnp.mean(x, axis=-1, keepdims=True)
    cen = x - mean
    inv = lax.rsqrt(jnp.mean(cen * cen, axis=-1, keepdims=True) + EPSILON)
    normed = cen * inv
    gate = u[...].astype(F32)
    gated = (normed * gate).astype(BF16)
    gated_o[...] = gated
    placing = (lax.broadcasted_iota(I32, (R, T), 0) == ints[0:1, :]).astype(BF16)
    gated_t = mm(placing, gated, TN).astype(BF16)
    picked = (mm(gated_t, w_out[...]) + ev_t[...]).astype(BF16)
    picked_o[...] = picked
    hidden = mm(picked, head_w1[...])
    active, slope = silu_parts(hidden)
    act_o[...] = active
    w2 = head_w2[...]
    relevance = jnp.sum(active * w2, axis=1, keepdims=True)
    observe = obs[:, :1]
    clicked = jnp.broadcast_to(ints[2:3, :], (T, T)).astype(F32).T[:, :1]
    rel_sig = jax.nn.sigmoid(relevance)
    obs_sig = jax.nn.sigmoid(observe)
    missing = jax.nn.sigmoid(-relevance) + rel_sig * jax.nn.sigmoid(-observe)
    d_rel = clicked * (rel_sig - 1.0) + (1.0 - clicked) * rel_sig * (1.0 - rel_sig) * obs_sig / missing
    d_obs = clicked * (obs_sig - 1.0) + (1.0 - clicked) * rel_sig * obs_sig * (1.0 - obs_sig) / missing
    drel_o[...] = jnp.broadcast_to(d_rel, (T, E))
    dobs_o[...] = jnp.broadcast_to(d_obs, (T, E))
    d_hidden = (d_rel * w2 * slope).astype(BF16)
    dhid_o[...] = d_hidden
    d_picked = mm(d_hidden, head_w1[...], NT).astype(BF16)
    d_out = (upstream[...].astype(F32) + mm(placing, d_picked)).astype(BF16)
    dout_o[...] = d_out
    d_gated = mm(d_out, w_out[...], NT)
    dpre_o[...] = (d_gated * normed * su[...].astype(F32)).astype(BF16)
    g = d_gated * gate
    first = jnp.mean(g, axis=-1, keepdims=True)
    second = jnp.mean(g * normed, axis=-1, keepdims=True)
    att[...] = inv * (g - first - normed * second)
    for k, ref in enumerate((d0, d1, d2, d3)):
        h = (y + k) & 3
        ref[...] = att[:, pl.ds(pl.multiple_of(h * E, E), E)].astype(BF16)


def packed(left, right):
    low = (lax.broadcasted_iota(I32, left.shape, 0) & 7) < 4
    n = left.shape[0]
    return jnp.where(low, left, pltpu.roll(right, 4, 0)), jnp.where(low, pltpu.roll(left, n - 4, 0), right)


def grads_kernel(
    meta, n0, dpre, gated, d_out, picked, d_hid, active, d_rel, d_obs, ints, emb, bpre, bias_w1, bias_w2,
    x_own, x_oth, s_own, s_oth,
):
    first = meta[3, 1] == 0

    def put(own_ref, oth_ref, col, left, right):
        x_0, x_1 = packed(left, right)
        cols = slice(col, col + left.shape[1])
        own_ref[:, cols] = jnp.where(first, x_0, x_1).astype(BF16)
        oth_ref[:, cols] = jnp.where(first, x_1, x_0).astype(BF16)

    g_u = mm(n0[...], dpre[...], TN)
    put(x_own, x_oth, 0, g_u[:, :256], g_u[:, 256:])
    g_wo = mm(gated[...], d_out[...], TN)
    put(x_own, x_oth, 256, g_wo[:, :256], g_wo[:, 256:])
    g_h1 = mm(picked[...], d_hid[...], TN)
    put(x_own, x_oth, 512, g_h1[:, :128], g_h1[:, 128:])
    hid, slope = silu_parts(bpre[...])
    d_bias = d_obs[...] * bias_w2[...] * slope
    g_b1 = mm(emb[...], d_bias, TN, HIGHEST)
    d_emb = mm(d_bias, bias_w1[...], NT, HIGHEST)
    pid = jnp.broadcast_to(ints[1:2, :], (2 * T, T))
    select_t = (lax.broadcasted_iota(I32, (2 * T, T), 0) == pid).astype(F32)
    g_tab = mm(select_t, d_emb, precision=HIGHEST)
    h2 = mm(active[...], d_rel[...], TN, HIGHEST)
    b2 = mm(hid, d_obs[...], TN, HIGHEST)
    lane2 = lax.broadcasted_iota(I32, (2 * T, E), 1)
    row2 = lax.broadcasted_iota(I32, (2 * T, E), 0)
    h2 = jnp.where(lane2 == (row2 & 1), h2, 0.0)
    b2 = jnp.where(lax.broadcasted_iota(I32, (T, E), 1) == 2, b2, 0.0)
    o2 = lax.broadcasted_iota(I32, (R, 2 * T), 0)
    i2 = lax.broadcasted_iota(I32, (R, 2 * T), 1)
    o1 = lax.broadcasted_iota(I32, (R, T), 0)
    i1 = lax.broadcasted_iota(I32, (R, T), 1)
    parts = []
    for cc in range(2):
        dest2 = 2 * (o2 >> 3) + cc
        dest1 = 2 * (o1 >> 3) + cc
        p_tab = (((o2 & 7) == 4) & (i2 == 2 * dest2)) | (((o2 & 7) == 5) & (i2 == 2 * dest2 + 1))
        p_h2 = ((o2 & 7) == 7) & ((i2 >> 1) == dest2)
        p_b1 = ((o1 & 7) == 6) & (i1 == dest1)
        p_b2 = ((o1 & 7) == 7) & (i1 == dest1)
        parts.append(
            mm(p_tab.astype(BF16), g_tab.astype(BF16))
            + mm(p_h2.astype(BF16), h2.astype(BF16))
            + mm(p_b1.astype(BF16), g_b1.astype(BF16))
            + mm(p_b2.astype(BF16), b2.astype(BF16))
        )
    s_own[...] = jnp.where(first, parts[0], parts[1]).astype(BF16)
    s_oth[...] = jnp.where(first, parts[1], parts[0]).astype(BF16)


def backward_kernel(
    meta, q_s, k_s, v_s, r0, r1, r2, r3, s_a, s_b, nt_a, nt_b, s_own, s_oth,
    x_own, x_oth,
    dq_s, dk_s, dv_s,
):
    y, core = meta[3, 0], meta[3, 1]
    dk_s[...] = jnp.zeros_like(dk_s)
    dv_s[...] = jnp.zeros_like(dv_s)
    rows = lax.broadcasted_iota(I32, (R, 1), 0)
    lanes = lax.broadcasted_iota(I32, (1, R), 1)
    for k, ref in enumerate((r0, r1, r2, r3)):
        blk = (y + 4 - k) & 3
        c = 2 * blk + core
        q = q_s[blk]
        g = ref[...]
        pos = lanes + c * R
        start = user_start(pos, meta)

        def step(b, dq, masked):
            kb = k_s[b]
            h = mm(kb, q, NT) * HALF
            dp = mm(v_s[b], g, NT)
            t = jnp.tanh(h)
            a = 1.0 + t
            w = h * a
            d = dp * (a + w * (1.0 - t))
            if masked:
                key_pos = rows + b * R
                keep = (key_pos >= start) & (key_pos <= pos)
                w = jnp.where(keep, w, 0.0)
                d = jnp.where(keep, d, 0.0)
            w = w.astype(BF16)
            d = d.astype(BF16)
            dv_s[b] += mm(w, g)
            dk_s[b] += mm(d, q)
            return dq + mm(d, kb, TN)

        first, full, diag, end = key_range(c * R, R, meta)
        acc = jnp.zeros((R, E), F32)
        acc = lax.fori_loop(first, full, functools.partial(step, masked=True), acc)
        acc = lax.fori_loop(full, diag, functools.partial(step, masked=False), acc)
        dq_s[blk] = lax.fori_loop(diag, end, functools.partial(step, masked=True), acc)
    g_q = jnp.zeros((W, E), F32)
    g_k = jnp.zeros((W, E), F32)
    g_v = jnp.zeros((W, E), F32)
    for i in range(4):
        b = 2 * i + core
        d = (dq_s[i] * HALF * s_a[i, :, :E].astype(F32)).astype(BF16)
        g_q = g_q + mm(nt_a[i], d)
        d = (dk_s[b] * HALF * s_a[i, :, E : 2 * E].astype(F32)).astype(BF16)
        g_k = g_k + mm(nt_a[i], d)
        d = (dv_s[b] * s_a[i, :, 2 * E :].astype(F32)).astype(BF16)
        g_v = g_v + mm(nt_a[i], d)
        b = 2 * i + 1 - core
        d = (dk_s[b] * HALF * s_b[i, :, :E].astype(F32)).astype(BF16)
        g_k = g_k + mm(nt_b[i], d)
        d = (dv_s[b] * s_b[i, :, E:].astype(F32)).astype(BF16)
        g_v = g_v + mm(nt_b[i], d)
    first = core == 0
    low = (lax.broadcasted_iota(I32, (W, E), 0) & 7) < 4
    x_0, x_1 = packed(g_q, g_k)
    x_own[:, :E] = jnp.where(first, x_0, x_1).astype(BF16)
    x_oth[:, :E] = jnp.where(first, x_1, x_0).astype(BF16)
    v_1 = pltpu.roll(g_v, W - 4, 0)
    x_own[:, E:] = jnp.where(low, jnp.where(first, g_v, v_1), s_own[...].astype(F32)).astype(BF16)
    x_oth[:, E:] = jnp.where(low, jnp.where(first, v_1, g_v), s_oth[...].astype(F32)).astype(BF16)


def sum_kernel(x_ref, g_in, g_out, g_h1, g_h2, g_tab, g_b1, g_b2):
    total = None
    for h in range(HEADS):
        part = jnp.zeros((8, 7 * E), F32)
        for i in range(16):
            at = (h * 16 + i) * 8
            part = part + x_ref[at : at + 8, :].astype(F32)
        g_in[:, W + h * E : W + (h + 1) * E] = part[0:4, 6 * E :]
        g_in[:, 2 * W + h * E : 2 * W + (h + 1) * E] = part[0:4, 5 * E : 6 * E]
        g_in[:, 3 * W + h * E : 3 * W + (h + 1) * E] = part[4:8, 5 * E : 6 * E]
        total = part if total is None else total + part
    g_in[:, 0:256] = total[0:4, 0:256]
    g_in[:, 256:512] = total[4:8, 0:256]
    g_out[:, 0:256] = total[0:4, 256:512]
    g_out[:, 256:512] = total[4:8, 256:512]
    g_h1[:, 0:128] = total[0:4, 512:640]
    g_h1[:, 128:256] = total[4:8, 512:640]
    g_tab[...] = total[4:6, 768:896]
    g_b1[...] = total[6:7, 768:896]
    g_h2[...] = total[7:8, 768:770]
    g_b2[...] = total[7:8, 770:771]


CHIPS = ("y", "xh", "xl", "z")
SWAP = []
for _i in range(32):
    _xh, _rest, _core = _i // 16, (_i // 2) % 8, _i % 2
    SWAP.append((_i, _i if _xh == _core else (1 - _xh) * 16 + _rest * 2 + 1 - _core))


def swapped(x):
    return lax.ppermute(x, ("xh", "xl", "z", "core"), SWAP)


def across(x):
    return lax.ppermute(x, "core", [(0, 1), (1, 0)])


def ring(x, k):
    return lax.ppermute(x, "y", [(i, (i + k) % 4) for i in range(4)])


def moved(x, axes, k):
    return lax.ppermute(x, axes, [(i, (i + k) % 4) for i in range(4)])


def tie(x, other):
    space = pl.BlockSpec(memory_space=pltpu.VMEM)
    return pl.pallas_call(
        lambda *_: None,
        out_shape=sds(x.shape, x.dtype),
        in_specs=[space] * 2,
        out_specs=space,
        compiler_params=pltpu.CompilerParams(vmem_limit_bytes=4 << 20),
        input_output_aliases={0: 0},
        name="tie",
    )(x, other)


def turned(x, k):
    return lax.ppermute(
        x, ("y", "core"), [(2 * i + c, 2 * ((i + (k if c == 0 else -k)) % 4) + c) for i in range(4) for c in range(2)]
    )


def body(
    events, lengths, target_rows, position_ids, labels, upstream,
    w_in, w_out, head_w1, head_w2, table, bias_w1, bias_w2,
):
    y, core = lax.axis_index("y"), lax.axis_index("core")
    w_rows = jnp.concatenate([w_in, w_out], axis=1)
    w_other = across(w_rows)
    w_rows = jnp.where(
        core == 0, jnp.concatenate([w_rows, w_other], axis=0), jnp.concatenate([w_other, w_rows], axis=0)
    )
    shared = jnp.where(core == 0, w_rows[:, :W], w_rows[:, 4 * W :])
    w_rows = jnp.concatenate([w_rows[:, W : 4 * W], shared], axis=1)
    x, z = 2 * lax.axis_index("xh") + lax.axis_index("xl"), lax.axis_index("z")
    line = [moved(w_rows, ("y",), k) for k in (3, 2, 1)]
    line = jnp.concatenate(line + [w_rows] + line, axis=0)
    line = lax.dynamic_slice_in_dim(line, ((3 - y) & 3) * 8, 32, 0)
    line = jnp.concatenate(
        [lax.dynamic_slice_in_dim(line, at + y * E, E, 1) for at in (W, 2 * W, 0)] + [line[:, 3 * W :]], axis=1
    )
    coords = jnp.stack([y, x, z]).astype(I32)
    (plane,) = call(
        plane_kernel,
        [sds((E, 7 * E), BF16)],
        [coords, line] + [moved(line, ("xh", "xl"), k) for k in (1, 2, 3)],
        limit=8,
        name="plane",
    )
    (wg,) = call(
        cube_kernel,
        [sds((W, 7 * E), BF16)],
        [coords, plane] + [moved(plane, ("z",), k) for k in (1, 2, 3)],
        scratch=[pltpu.VMEM((W, 7 * E), F32)],
        limit=12,
        name="cube",
    )

    ev = swapped(events[0])
    place = jnp.stack([y, lax.axis_index("xh")]).astype(I32)[None]
    line = jnp.pad(jnp.concatenate([place, lengths], axis=1), ((0, 0), (0, T - 6)))
    ints = swapped(jnp.concatenate([target_rows, position_ids, labels, line], axis=0))
    meta = ints
    (n0,) = call(norm_kernel, [sds((R, W), BF16)], [ev, line], n_smem=0, n_any=1, limit=12, name="norm")
    na = turned(n0, 1)
    nb = turned(n0, 3)
    na = tie(na, plane)
    nc = turned(na, 1)
    n0, nb, na = tie(n0, wg), tie(nb, wg), tie(na, nc)
    parts = [n0, na, nb, nc]
    parts = parts + [across(p) for p in parts]
    up = swapped(upstream[0])

    qkv = [sds((4, R, E), BF16), sds((8, R, E), BF16), sds((8, R, E), BF16)]
    a0, a1, a2, a3, q_s, k_s, v_s = call(
        forward_kernel, [sds((R + 16, E), BF16)] * 4 + qkv, [meta] + parts + [wg], flops=5 * 10**9, name="forward"
    )
    r1, r2, r3 = ring(a1, 1), ring(a2, 2), ring(a3, 3)
    wg = tie(wg, a0)
    w_half = across(wg[:, 3 * E :])
    u, su, w_o, ev_t, emb, bpre, obs = call(
        side_kernel,
        [sds((R, W), BF16)] * 3 + [sds((T, W), F32)] + [sds((T, E), F32)] * 3,
        [meta, n0, wg, w_half, ev, ints, table, bias_w1, bias_w2.reshape(1, E)],
        flops=10**9,
        name="side",
    )

    def slopes(width, blocks, after):
        return call(
            slopes_kernel,
            [sds((4, R, width), BF16), sds((4, W, R), BF16)],
            [meta] + blocks + [wg, after],
            n_any=1,
            flops=10**9,
            name="slopes",
        )

    s_a, nt_a = slopes(3 * E, parts[:4], a0)
    w2 = head_w2.reshape(1, 2 * E)
    b2 = bias_w2.reshape(1, E)
    d0, d1, d2, d3, gated, d_out, dpre, picked, d_hid, active, d_rel, d_obs = call(
        middle_kernel,
        [sds((R, E), BF16)] * 4
        + [sds((R, W), BF16)] * 3
        + [sds((T, W), BF16), sds((T, 2 * E), BF16), sds((T, 2 * E), F32), sds((T, E), F32), sds((T, E), F32)],
        [meta, a0, r1, r2, r3, u, su, w_o, ev_t, obs, ints, up, head_w1, w2],
        scratch=[pltpu.VMEM((R, W), F32)],
        flops=10**9,
        name="middle",
    )
    g1, g2, g3 = ring(d1, 1), ring(d2, 2), ring(d3, 3)
    s_b, nt_b = slopes(2 * E, parts[4:], d0)
    early, early_oth, s_own, s_oth = call(
        grads_kernel,
        [sds((R, 5 * E), BF16)] * 2 + [sds((R, E), BF16)] * 2,
        [meta, n0, dpre, gated, d_out, picked, d_hid, active, d_rel, d_obs, ints, emb, bpre, bias_w1, b2],
        flops=2 * 10**9,
        name="grads",
    )
    early_in = across(early_oth)
    late, late_oth = call(
        backward_kernel,
        [sds((R, 2 * E), BF16)] * 2,
        [meta, q_s, k_s, v_s, d0, g1, g2, g3, s_a, s_b, nt_a, nt_b, s_own, s_oth],
        scratch=[pltpu.VMEM((4, R, E), F32), pltpu.VMEM((8, R, E), F32), pltpu.VMEM((8, R, E), F32)],
        flops=10**10,
        limit=28,
        name="backward",
    )
    late_in = across(late_oth)
    pair = jnp.concatenate(
        [
            (early.astype(F32) + early_in.astype(F32)).astype(BF16),
            (late.astype(F32) + late_in.astype(F32)).astype(BF16),
        ],
        axis=1,
    )
    got = lax.all_to_all(pair, CHIPS, 0, 0, tiled=True)
    g_in, g_out, g_h1, g_h2, g_tab, g_b1, g_b2 = call(
        sum_kernel,
        [sds((4, 4 * W), F32), sds((4, W), F32), sds((4, 2 * E), F32)]
        + [sds((1, 2), F32), sds((2, E), F32), sds((1, E), F32), sds((1, 1), F32)],
        [got],
        n_smem=0,
        name="total",
    )
    return g_in, g_out, g_h1, g_h2.reshape(2), g_tab, g_b1, g_b2.reshape(1)


def solution(mesh):
    fine = Mesh(mesh.devices.reshape(4, 2, 2, 4, 2), ("y", "xh", "xl", "z", "core"))
    ctx, dp = ("y", "xh"), ("xl", "z", "core")
    every = ctx + dp
    in_specs = (
        P(dp, ctx, None),
        P(dp, None),
        P(dp, ctx),
        P(dp, ctx),
        P(dp, ctx),
        P(dp, ctx, None),
        P(every, None),
        P(every, None),
        P(),
        P(),
        P(),
        P(),
        P(),
    )
    out_specs = (
        P(every, None),
        P(every, None),
        P(every, None),
        P(every),
        P(every, None),
        P(every, None),
        P(every),
    )
    return jax.shard_map(body, mesh=fine, in_specs=in_specs, out_specs=out_specs, check_vma=False)
```

```python
import functools
import math

import jax
import jax.numpy as jnp
from jax import lax
from jax.experimental import pallas as pl
from jax.experimental.pallas import tpu as pltpu
from jax.sharding import Mesh, PartitionSpec as P

HEADS = 4
EPSILON = 1e-05
HIGHEST = lax.Precision.HIGHEST
F32 = jnp.float32
BF16 = jnp.bfloat16
I32 = jnp.int32
R = 512
W = 512
E = 128
T = 128
SCALE = 1.0 / math.sqrt(E)
HALF = 0.5 * SCALE

NN = (((1,), (0,)), ((), ()))
NT = (((1,), (1,)), ((), ()))
TN = (((0,), (0,)), ((), ()))


def mm(a, b, dims=NN, precision=None):
    return lax.dot_general(a, b, dims, precision=precision, preferred_element_type=F32)


def silu_parts(z):
    h = 0.5 * z
    t = jnp.tanh(h)
    a = 1.0 + t
    w = h * a
    return w, 0.5 * (a + w * (1.0 - t))


def silu(z):
    h = 0.5 * z
    return h + h * jnp.tanh(h)


def vmem(n):
    return [pl.BlockSpec(memory_space=pltpu.VMEM)] * n


def smem():
    return [pl.BlockSpec(memory_space=pltpu.SMEM)]


def call(kernel, outs, args, scratch=(), limit=24, flops=0, n_smem=1, n_any=0, name=None):
    total = sum(a.size * a.dtype.itemsize for a in args) + sum(
        math.prod(o.shape) * o.dtype.itemsize for o in outs
    )
    return pl.pallas_call(
        kernel,
        out_shape=tuple(outs),
        in_specs=smem() * n_smem
        + vmem(len(args) - n_smem - n_any)
        + [pl.BlockSpec(memory_space=pl.ANY)] * n_any,
        out_specs=tuple(vmem(len(outs))),
        scratch_shapes=list(scratch),
        compiler_params=pltpu.CompilerParams(vmem_limit_bytes=limit << 20),
        cost_estimate=pl.CostEstimate(flops=flops, bytes_accessed=total, transcendentals=0),
        name=name,
    )(*args)


def sds(shape, dtype):
    return jax.ShapeDtypeStruct(shape, dtype)


def plane_kernel(coords, q0, q1, q2, q3, out):
    for k, ref in enumerate((q0, q1, q2, q3)):
        out[pl.ds(pl.multiple_of(((coords[1] + 4 - k) & 3) * 32, 32), 32), :] = ref[...]


def cube_kernel(coords, q0, q1, q2, q3, out, half, rows):
    for k, ref in enumerate((q0, q1, q2, q3)):
        z = ((coords[2] + 4 - k) & 3) * 8
        part = ref[...].astype(F32)
        for i in range(4):
            for j in range(4):
                at = i * 32 + j * 8
                rows[pl.ds(pl.multiple_of(j * E + i * 32 + z, 8), 8), :] = part[at : at + 8]
    out[...] = rows[:, : 3 * E].astype(BF16)
    half[...] = rows[:, 3 * E :].astype(BF16)


def norm_kernel(x_ref, _, o_ref):
    x = x_ref[...].astype(F32)
    mean = jnp.mean(x, axis=-1, keepdims=True)
    cen = x - mean
    inv = lax.rsqrt(jnp.mean(cen * cen, axis=-1, keepdims=True) + EPSILON)
    o_ref[...] = (cen * inv).astype(BF16)


def user_start(pos, meta):
    start = jnp.zeros_like(pos)
    end = 0
    for j in range(3):
        end = end + meta[3, 2 + j]
        start = jnp.where(pos >= end, end, start)
    return start


def places(y, core):
    s = jnp.where(core == 0, 3, 1)
    back, on, far = (y + s) & 3, (y + 4 - s) & 3, (y + 2) & 3
    return (y, back, on, far), (y, on, back, far)


def key_range(base, rows, meta):
    lo = user_start(base, meta)
    last = base + rows - 1
    end = last // R + 1
    first = lo // R
    diag = base // R
    full = jnp.clip((user_start(last, meta) + R - 1) // R, first, diag)
    return first, full, diag, end


def forward_kernel(meta, n0, na, nb, nc, o0, oa, ob, oc, wg, a0, a1, a2, a3, q_s, k_s, v_s):
    y, core = meta[3, 0], meta[3, 1]
    own, oth = places(y, core)
    for blk, ref in zip(own, (n0, na, nb, nc)):
        b = 2 * blk + core
        p = silu(mm(ref[...], wg[:, : 3 * E])).astype(BF16)
        q_s[blk] = p[:, :E]
        k_s[b] = p[:, E : 2 * E]
        v_s[b] = p[:, 2 * E :]
    for blk, ref in zip(oth, (o0, oa, ob, oc)):
        b = 2 * blk + 1 - core
        p = silu(mm(ref[...], wg[:, E : 3 * E])).astype(BF16)
        k_s[b] = p[:, :E]
        v_s[b] = p[:, E:]
    rows = lax.broadcasted_iota(I32, (R, 1), 0)
    lanes = lax.broadcasted_iota(I32, (1, R), 1)
    for k, out in enumerate((a0, a1, a2, a3)):
        blk = (y + k) & 3
        c = 2 * blk + core
        q = q_s[blk]
        pos = rows + c * R
        start = user_start(pos, meta)

        def step(b, acc, masked):
            h = mm(q, k_s[b], NT) * HALF
            w = h + h * jnp.tanh(h)
            if masked:
                key_pos = lanes + b * R
                w = jnp.where((key_pos >= start) & (key_pos <= pos), w, 0.0)
            return acc + mm(w.astype(BF16), v_s[b])

        first, full, diag, end = key_range(c * R, R, meta)
        acc = jnp.zeros((R, E), F32)
        acc = lax.fori_loop(first, full, functools.partial(step, masked=True), acc)
        acc = lax.fori_loop(full, diag, functools.partial(step, masked=False), acc)
        acc = lax.fori_loop(diag, end, functools.partial(step, masked=True), acc)
        mean = jnp.mean(acc, axis=-1, keepdims=True).astype(BF16)
        out[:R] = (acc - mean.astype(F32)).astype(BF16)
        one = (lax.broadcasted_iota(I32, (16, E), 1) == 0).astype(BF16)
        line = mm(one, jnp.broadcast_to(mean, (R, E)), NT)
        out[R:] = jnp.concatenate(
            [line[0:1, i * E : (i + 1) * E] for i in range(4)] + [jnp.zeros((12, E), F32)], axis=0
        ).astype(BF16)


def side_kernel(
    meta, n0, w_mine, wo_half, events, ints, table, bias_w1, bias_w2, u, su, w_out, ev_t, emb, bpre, obs
):
    first = meta[3, 1] == 0
    mine = w_mine[...]
    other = wo_half[...]
    w_u = jnp.where(first, mine, other)
    w_out[...] = jnp.where(first, other, mine)
    act, slope = silu_parts(mm(n0[...], w_u))
    u[...] = act.astype(BF16)
    su[...] = slope.astype(BF16)
    placing = (lax.broadcasted_iota(I32, (R, T), 0) == ints[0:1, :]).astype(BF16)
    ev_t[...] = mm(placing, events[...], TN)
    pid = jnp.broadcast_to(ints[1:2, :], (T, T)).astype(F32).T.astype(I32)
    pid = jnp.concatenate([pid, pid], axis=1)
    selector = (lax.broadcasted_iota(I32, (T, 2 * T), 1) == pid).astype(F32)
    embedded = mm(selector, table[...], precision=HIGHEST)
    bias_pre = mm(embedded, bias_w1[...], precision=HIGHEST)
    emb[...] = embedded
    bpre[...] = bias_pre
    hid = silu(bias_pre)
    obs[...] = jnp.broadcast_to(jnp.sum(hid * bias_w2[...], axis=1, keepdims=True), (T, E))


def slopes_kernel(meta, n0, na, nb, nc, wg, _, s_o, nt, kt):
    y, core = meta[3, 0], meta[3, 1]
    width = s_o.shape[2]
    own, oth = places(y, core)
    for blk, ref in zip(own if width == 3 * E else oth, (n0, na, nb, nc)):
        x = ref[...]
        act, slope = silu_parts(mm(x, wg[:, 3 * E - width : 3 * E]))
        s_o[blk] = slope.astype(BF16)
        kt[blk] = act[:, width - 2 * E : width - E].astype(BF16).T
        nt[blk] = x.T


def middle_kernel(
    meta, r0, r1, r2, r3, u, su, w_out, ev_t, obs, ints, upstream, head_w1, head_w2,
    d0, d1, d2, d3, gated_o, dout_o, dpre_o, picked_o, dhid_o, act_o, drel_o, dobs_o,
    att,
):
    y = meta[3, 0]
    for k, ref in enumerate((r0, r1, r2, r3)):
        h = (y + 4 - k) & 3
        means = ref[R:]
        pick = lax.broadcasted_iota(I32, (16, E), 0)
        column = jnp.concatenate([mm(means, (pick == i).astype(BF16), TN) for i in range(4)], axis=0)
        att[:, pl.ds(pl.multiple_of(h * E, E), E)] = ref[:R].astype(F32) + column
    x = att[...]
    mean = jnp.mean(x, axis=-1, keepdims=True)
    cen = x - mean
    inv = lax.rsqrt(jnp.mean(cen * cen, axis=-1, keepdims=True) + EPSILON)
    normed = cen * inv
    gate = u[...].astype(F32)
    gated = (normed * gate).astype(BF16)
    gated_o[...] = gated
    placing = (lax.broadcasted_iota(I32, (R, T), 0) == ints[0:1, :]).astype(BF16)
    gated_t = mm(placing, gated, TN).astype(BF16)
    picked = (mm(gated_t, w_out[...]) + ev_t[...]).astype(BF16)
    picked_o[...] = picked
    hidden = mm(picked, head_w1[...])
    active, slope = silu_parts(hidden)
    act_o[...] = active
    w2 = head_w2[...]
    relevance = jnp.sum(active * w2, axis=1, keepdims=True)
    observe = obs[:, :1]
    clicked = jnp.broadcast_to(ints[2:3, :], (T, T)).astype(F32).T[:, :1]
    rel_sig = jax.nn.sigmoid(relevance)
    obs_sig = jax.nn.sigmoid(observe)
    missing = jax.nn.sigmoid(-relevance) + rel_sig * jax.nn.sigmoid(-observe)
    d_rel = clicked * (rel_sig - 1.0) + (1.0 - clicked) * rel_sig * (1.0 - rel_sig) * obs_sig / missing
    d_obs = clicked * (obs_sig - 1.0) + (1.0 - clicked) * rel_sig * obs_sig * (1.0 - obs_sig) / missing
    drel_o[...] = jnp.broadcast_to(d_rel, (T, E))
    dobs_o[...] = jnp.broadcast_to(d_obs, (T, E))
    d_hidden = (d_rel * w2 * slope).astype(BF16)
    dhid_o[...] = d_hidden
    d_picked = mm(d_hidden, head_w1[...], NT).astype(BF16)
    d_out = (upstream[...].astype(F32) + mm(placing, d_picked)).astype(BF16)
    dout_o[...] = d_out
    d_gated = mm(d_out, w_out[...], NT)
    dpre_o[...] = (d_gated * normed * su[...].astype(F32)).astype(BF16)
    g = d_gated * gate
    first = jnp.mean(g, axis=-1, keepdims=True)
    second = jnp.mean(g * normed, axis=-1, keepdims=True)
    att[...] = inv * (g - first - normed * second)
    for k, ref in enumerate((d0, d1, d2, d3)):
        h = (y + k) & 3
        ref[...] = att[:, pl.ds(pl.multiple_of(h * E, E), E)].astype(BF16)


def packed(left, right):
    low = (lax.broadcasted_iota(I32, left.shape, 0) & 7) < 4
    n = left.shape[0]
    return jnp.where(low, left, pltpu.roll(right, 4, 0)), jnp.where(low, pltpu.roll(left, n - 4, 0), right)


def grads_kernel(
    meta, n0, dpre, gated, d_out, picked, d_hid, active, d_rel, d_obs, ints, emb, bpre, bias_w1, bias_w2,
    x_own, x_oth, s_own, s_oth,
):
    first = meta[3, 1] == 0

    def put(own_ref, oth_ref, col, left, right):
        x_0, x_1 = packed(left, right)
        cols = slice(col, col + left.shape[1])
        own_ref[:, cols] = jnp.where(first, x_0, x_1).astype(BF16)
        oth_ref[:, cols] = jnp.where(first, x_1, x_0).astype(BF16)

    g_u = mm(n0[...], dpre[...], TN)
    put(x_own, x_oth, 0, g_u[:, :256], g_u[:, 256:])
    g_wo = mm(gated[...], d_out[...], TN)
    put(x_own, x_oth, 256, g_wo[:, :256], g_wo[:, 256:])
    g_h1 = mm(picked[...], d_hid[...], TN)
    put(x_own, x_oth, 512, g_h1[:, :128], g_h1[:, 128:])
    hid, slope = silu_parts(bpre[...])
    d_bias = d_obs[...] * bias_w2[...] * slope
    g_b1 = mm(emb[...], d_bias, TN, HIGHEST)
    d_emb = mm(d_bias, bias_w1[...], NT, HIGHEST)
    pid = jnp.broadcast_to(ints[1:2, :], (2 * T, T))
    select_t = (lax.broadcasted_iota(I32, (2 * T, T), 0) == pid).astype(F32)
    g_tab = mm(select_t, d_emb, precision=HIGHEST)
    h2 = mm(active[...], d_rel[...], TN, HIGHEST)
    b2 = mm(hid, d_obs[...], TN, HIGHEST)
    lane2 = lax.broadcasted_iota(I32, (2 * T, E), 1)
    row2 = lax.broadcasted_iota(I32, (2 * T, E), 0)
    h2 = jnp.where(lane2 == (row2 & 1), h2, 0.0)
    b2 = jnp.where(lax.broadcasted_iota(I32, (T, E), 1) == 2, b2, 0.0)
    o2 = lax.broadcasted_iota(I32, (R, 2 * T), 0)
    i2 = lax.broadcasted_iota(I32, (R, 2 * T), 1)
    o1 = lax.broadcasted_iota(I32, (R, T), 0)
    i1 = lax.broadcasted_iota(I32, (R, T), 1)
    parts = []
    for cc in range(2):
        dest2 = 2 * (o2 >> 3) + cc
        dest1 = 2 * (o1 >> 3) + cc
        p_tab = (((o2 & 7) == 4) & (i2 == 2 * dest2)) | (((o2 & 7) == 5) & (i2 == 2 * dest2 + 1))
        p_h2 = ((o2 & 7) == 7) & ((i2 >> 1) == dest2)
        p_b1 = ((o1 & 7) == 6) & (i1 == dest1)
        p_b2 = ((o1 & 7) == 7) & (i1 == dest1)
        parts.append(
            mm(p_tab.astype(BF16), g_tab.astype(BF16))
            + mm(p_h2.astype(BF16), h2.astype(BF16))
            + mm(p_b1.astype(BF16), g_b1.astype(BF16))
            + mm(p_b2.astype(BF16), b2.astype(BF16))
        )
    s_own[...] = jnp.where(first, parts[0], parts[1]).astype(BF16)
    s_oth[...] = jnp.where(first, parts[1], parts[0]).astype(BF16)


def backward_kernel(
    meta, q_s, k_s, v_s, r0, r1, r2, r3, s_a, s_b, nt_a, nt_b, kt_a, kt_b, s_own, s_oth,
    x_own, x_oth,
    dq_s, dk_s, dv_s, kt_s,
):
    y, core = meta[3, 0], meta[3, 1]
    for i in range(4):
        kt_s[2 * i + core] = kt_a[i]
        kt_s[2 * i + 1 - core] = kt_b[i]
    dk_s[...] = jnp.zeros_like(dk_s)
    dv_s[...] = jnp.zeros_like(dv_s)
    rows = lax.broadcasted_iota(I32, (R, 1), 0)
    lanes = lax.broadcasted_iota(I32, (1, R), 1)
    for k, ref in enumerate((r0, r1, r2, r3)):
        blk = (y + 4 - k) & 3
        c = 2 * blk + core
        q = q_s[blk]
        g = ref[...]
        pos = lanes + c * R
        start = user_start(pos, meta)

        def step(b, dq, masked):
            kb = k_s[b]
            h = mm(kb, q, NT) * HALF
            dp = mm(v_s[b], g, NT)
            t = jnp.tanh(h)
            a = 1.0 + t
            w = h * a
            d = dp * (a + w * (1.0 - t))
            if masked:
                key_pos = rows + b * R
                keep = (key_pos >= start) & (key_pos <= pos)
                w = jnp.where(keep, w, 0.0)
                d = jnp.where(keep, d, 0.0)
            w = w.astype(BF16)
            d = d.astype(BF16)
            dv_s[b] += mm(w, g)
            dk_s[b] += mm(d, q)
            return dq + mm(kt_s[b], d)

        first, full, diag, end = key_range(c * R, R, meta)
        acc = jnp.zeros((E, R), F32)
        acc = lax.fori_loop(first, full, functools.partial(step, masked=True), acc)
        acc = lax.fori_loop(full, diag, functools.partial(step, masked=False), acc)
        acc = lax.fori_loop(diag, end, functools.partial(step, masked=True), acc)
        dq_s[blk] = acc.T
    g_all = jnp.zeros((W, 3 * E), F32)
    g_kv = jnp.zeros((W, 2 * E), F32)
    for i in range(4):
        b = 2 * i + core
        d = jnp.concatenate([dq_s[i] * HALF, dk_s[b] * HALF, dv_s[b]], axis=1) * s_a[i].astype(F32)
        g_all = g_all + mm(nt_a[i], d.astype(BF16))
        b = 2 * i + 1 - core
        d = jnp.concatenate([dk_s[b] * HALF, dv_s[b]], axis=1) * s_b[i].astype(F32)
        g_kv = g_kv + mm(nt_b[i], d.astype(BF16))
    g_q = g_all[:, :E]
    g_k = g_all[:, E : 2 * E] + g_kv[:, :E]
    g_v = g_all[:, 2 * E :] + g_kv[:, E:]
    first = core == 0
    low = (lax.broadcasted_iota(I32, (W, E), 0) & 7) < 4
    x_0, x_1 = packed(g_q, g_k)
    x_own[:, :E] = jnp.where(first, x_0, x_1).astype(BF16)
    x_oth[:, :E] = jnp.where(first, x_1, x_0).astype(BF16)
    v_1 = pltpu.roll(g_v, W - 4, 0)
    x_own[:, E:] = jnp.where(low, jnp.where(first, g_v, v_1), s_own[...].astype(F32)).astype(BF16)
    x_oth[:, E:] = jnp.where(low, jnp.where(first, v_1, g_v), s_oth[...].astype(F32)).astype(BF16)


def sum_kernel(x_ref, g_in, g_out, g_h1, g_h2, g_tab, g_b1, g_b2):
    total = None
    for h in range(HEADS):
        part = jnp.zeros((8, 7 * E), F32)
        for i in range(16):
            at = (h * 16 + i) * 8
            part = part + x_ref[at : at + 8, :].astype(F32)
        g_in[:, W + h * E : W + (h + 1) * E] = part[0:4, 6 * E :]
        g_in[:, 2 * W + h * E : 2 * W + (h + 1) * E] = part[0:4, 5 * E : 6 * E]
        g_in[:, 3 * W + h * E : 3 * W + (h + 1) * E] = part[4:8, 5 * E : 6 * E]
        total = part if total is None else total + part
    g_in[:, 0:256] = total[0:4, 0:256]
    g_in[:, 256:512] = total[4:8, 0:256]
    g_out[:, 0:256] = total[0:4, 256:512]
    g_out[:, 256:512] = total[4:8, 256:512]
    g_h1[:, 0:128] = total[0:4, 512:640]
    g_h1[:, 128:256] = total[4:8, 512:640]
    g_tab[...] = total[4:6, 768:896]
    g_b1[...] = total[6:7, 768:896]
    g_h2[...] = total[7:8, 768:770]
    g_b2[...] = total[7:8, 770:771]


CHIPS = ("y", "xh", "xl", "z")
SWAP = []
for _i in range(32):
    _xh, _rest, _core = _i // 16, (_i // 2) % 8, _i % 2
    SWAP.append((_i, _i if _xh == _core else (1 - _xh) * 16 + _rest * 2 + 1 - _core))


def swapped(x):
    return lax.ppermute(x, ("xh", "xl", "z", "core"), SWAP)


def across(x):
    return lax.ppermute(x, "core", [(0, 1), (1, 0)])


def ring(x, k):
    return lax.ppermute(x, "y", [(i, (i + k) % 4) for i in range(4)])


def moved(x, axes, k):
    return lax.ppermute(x, axes, [(i, (i + k) % 4) for i in range(4)])


def tie(x, other):
    space = pl.BlockSpec(memory_space=pltpu.VMEM)
    return pl.pallas_call(
        lambda *_: None,
        out_shape=sds(x.shape, x.dtype),
        in_specs=[space] * 2,
        out_specs=space,
        compiler_params=pltpu.CompilerParams(vmem_limit_bytes=4 << 20),
        input_output_aliases={0: 0},
        name="tie",
    )(x, other)


def turned(x, k):
    return lax.ppermute(
        x, ("y", "core"), [(2 * i + c, 2 * ((i + (k if c == 0 else -k)) % 4) + c) for i in range(4) for c in range(2)]
    )


def body(
    events, lengths, target_rows, position_ids, labels, upstream,
    w_in, w_out, head_w1, head_w2, table, bias_w1, bias_w2,
):
    y, core = lax.axis_index("y"), lax.axis_index("core")
    w_rows = jnp.concatenate([w_in, w_out], axis=1)
    w_other = across(w_rows)
    w_rows = jnp.where(
        core == 0, jnp.concatenate([w_rows, w_other], axis=0), jnp.concatenate([w_other, w_rows], axis=0)
    )
    shared = jnp.where(core == 0, w_rows[:, :W], w_rows[:, 4 * W :])
    w_rows = jnp.concatenate([w_rows[:, W : 4 * W], shared], axis=1)
    x, z = 2 * lax.axis_index("xh") + lax.axis_index("xl"), lax.axis_index("z")
    line = [moved(w_rows, ("y",), k) for k in (3, 2, 1)]
    line = jnp.concatenate(line + [w_rows] + line, axis=0)
    line = lax.dynamic_slice_in_dim(line, ((3 - y) & 3) * 8, 32, 0)
    line = jnp.concatenate(
        [lax.dynamic_slice_in_dim(line, at + y * E, E, 1) for at in (W, 2 * W, 0)] + [line[:, 3 * W :]], axis=1
    )
    coords = jnp.stack([y, x, z]).astype(I32)
    (plane,) = call(
        plane_kernel,
        [sds((E, 7 * E), BF16)],
        [coords, line] + [moved(line, ("xh", "xl"), k) for k in (1, 2, 3)],
        limit=8,
        name="plane",
    )
    wg, w_mine = call(
        cube_kernel,
        [sds((W, 3 * E), BF16), sds((W, W), BF16)],
        [coords, plane] + [moved(plane, ("z",), k) for k in (1, 2, 3)],
        scratch=[pltpu.VMEM((W, 7 * E), F32)],
        limit=12,
        name="cube",
    )

    w_half = across(w_mine)

    ev = swapped(events[0])
    place = jnp.stack([y, lax.axis_index("xh")]).astype(I32)[None]
    line = jnp.pad(jnp.concatenate([place, lengths], axis=1), ((0, 0), (0, T - 6)))
    ints = swapped(jnp.concatenate([target_rows, position_ids, labels, line], axis=0))
    meta = ints
    (n0,) = call(norm_kernel, [sds((R, W), BF16)], [ev, line], n_smem=0, n_any=1, limit=12, name="norm")
    na = turned(n0, 1)
    nb = turned(n0, 3)
    na = tie(na, plane)
    nc = turned(na, 1)
    n0, nb, na = tie(n0, wg), tie(nb, wg), tie(na, nc)
    parts = [n0, na, nb, nc]
    parts = parts + [across(p) for p in parts]
    up = swapped(upstream[0])

    qkv = [sds((4, R, E), BF16), sds((8, R, E), BF16), sds((8, R, E), BF16)]
    a0, a1, a2, a3, q_s, k_s, v_s = call(
        forward_kernel, [sds((R + 16, E), BF16)] * 4 + qkv, [meta] + parts + [wg], flops=5 * 10**9, name="forward"
    )
    r1, r2, r3 = ring(a1, 1), ring(a2, 2), ring(a3, 3)
    u, su, w_o, ev_t, emb, bpre, obs = call(
        side_kernel,
        [sds((R, W), BF16)] * 3 + [sds((T, W), F32)] + [sds((T, E), F32)] * 3,
        [meta, n0, w_mine, w_half, ev, ints, table, bias_w1, bias_w2.reshape(1, E)],
        flops=10**9,
        name="side",
    )

    def slopes(width, blocks, after):
        return call(
            slopes_kernel,
            [sds((4, R, width), BF16), sds((4, W, R), BF16), sds((4, E, R), BF16)],
            [meta] + blocks + [wg, after],
            n_any=1,
            flops=10**9,
            name="slopes",
        )

    s_a, nt_a, kt_a = slopes(3 * E, parts[:4], a0)
    w2 = head_w2.reshape(1, 2 * E)
    b2 = bias_w2.reshape(1, E)
    d0, d1, d2, d3, gated, d_out, dpre, picked, d_hid, active, d_rel, d_obs = call(
        middle_kernel,
        [sds((R, E), BF16)] * 4
        + [sds((R, W), BF16)] * 3
        + [sds((T, W), BF16), sds((T, 2 * E), BF16), sds((T, 2 * E), F32), sds((T, E), F32), sds((T, E), F32)],
        [meta, a0, r1, r2, r3, u, su, w_o, ev_t, obs, ints, up, head_w1, w2],
        scratch=[pltpu.VMEM((R, W), F32)],
        flops=10**9,
        name="middle",
    )
    g1, g2, g3 = ring(d1, 1), ring(d2, 2), ring(d3, 3)
    s_b, nt_b, kt_b = slopes(2 * E, parts[4:], d0)
    early, early_oth, s_own, s_oth = call(
        grads_kernel,
        [sds((R, 5 * E), BF16)] * 2 + [sds((R, E), BF16)] * 2,
        [meta, n0, dpre, gated, d_out, picked, d_hid, active, d_rel, d_obs, ints, emb, bpre, bias_w1, b2],
        flops=2 * 10**9,
        name="grads",
    )
    early_in = across(early_oth)
    late, late_oth = call(
        backward_kernel,
        [sds((R, 2 * E), BF16)] * 2,
        [meta, q_s, k_s, v_s, d0, g1, g2, g3, s_a, s_b, nt_a, nt_b, kt_a, kt_b, s_own, s_oth],
        scratch=[pltpu.VMEM((4, R, E), F32), pltpu.VMEM((8, R, E), F32), pltpu.VMEM((8, R, E), F32)]
        + [pltpu.VMEM((8, E, R), BF16)],
        flops=10**10,
        limit=28,
        name="backward",
    )
    late_in = across(late_oth)
    pair = jnp.concatenate(
        [
            (early.astype(F32) + early_in.astype(F32)).astype(BF16),
            (late.astype(F32) + late_in.astype(F32)).astype(BF16),
        ],
        axis=1,
    )
    got = lax.all_to_all(pair, CHIPS, 0, 0, tiled=True)
    g_in, g_out, g_h1, g_h2, g_tab, g_b1, g_b2 = call(
        sum_kernel,
        [sds((4, 4 * W), F32), sds((4, W), F32), sds((4, 2 * E), F32)]
        + [sds((1, 2), F32), sds((2, E), F32), sds((1, E), F32), sds((1, 1), F32)],
        [got],
        n_smem=0,
        name="total",
    )
    return g_in, g_out, g_h1, g_h2.reshape(2), g_tab, g_b1, g_b2.reshape(1)


def solution(mesh):
    fine = Mesh(mesh.devices.reshape(4, 2, 2, 4, 2), ("y", "xh", "xl", "z", "core"))
    ctx, dp = ("y", "xh"), ("xl", "z", "core")
    every = ctx + dp
    in_specs = (
        P(dp, ctx, None),
        P(dp, None),
        P(dp, ctx),
        P(dp, ctx),
        P(dp, ctx),
        P(dp, ctx, None),
        P(every, None),
        P(every, None),
        P(),
        P(),
        P(),
        P(),
        P(),
    )
    out_specs = (
        P(every, None),
        P(every, None),
        P(every, None),
        P(every),
        P(every, None),
        P(every, None),
        P(every),
    )
    return jax.shard_map(body, mesh=fine, in_specs=in_specs, out_specs=out_specs, check_vma=False)
```

```python
import functools
import math

import jax
import jax.numpy as jnp
from jax import lax
from jax.experimental import pallas as pl
from jax.experimental.pallas import tpu as pltpu
from jax.sharding import Mesh, PartitionSpec as P

HEADS = 4
EPSILON = 1e-05
HIGHEST = lax.Precision.HIGHEST
F32 = jnp.float32
BF16 = jnp.bfloat16
I32 = jnp.int32
R = 512
W = 512
E = 128
T = 128
SCALE = 1.0 / math.sqrt(E)
HALF = 0.5 * SCALE

NN = (((1,), (0,)), ((), ()))
NT = (((1,), (1,)), ((), ()))
TN = (((0,), (0,)), ((), ()))


def mm(a, b, dims=NN, precision=None):
    return lax.dot_general(a, b, dims, precision=precision, preferred_element_type=F32)


def silu_parts(z):
    h = 0.5 * z
    t = jnp.tanh(h)
    a = 1.0 + t
    w = h * a
    return w, 0.5 * (a + w * (1.0 - t))


def silu(z):
    h = 0.5 * z
    return h + h * jnp.tanh(h)


def vmem(n):
    return [pl.BlockSpec(memory_space=pltpu.VMEM)] * n


def smem():
    return [pl.BlockSpec(memory_space=pltpu.SMEM)]


def call(kernel, outs, args, scratch=(), limit=24, flops=0, n_smem=1, n_any=0, name=None):
    total = sum(a.size * a.dtype.itemsize for a in args) + sum(
        math.prod(o.shape) * o.dtype.itemsize for o in outs
    )
    return pl.pallas_call(
        kernel,
        out_shape=tuple(outs),
        in_specs=smem() * n_smem
        + vmem(len(args) - n_smem - n_any)
        + [pl.BlockSpec(memory_space=pl.ANY)] * n_any,
        out_specs=tuple(vmem(len(outs))),
        scratch_shapes=list(scratch),
        compiler_params=pltpu.CompilerParams(vmem_limit_bytes=limit << 20),
        cost_estimate=pl.CostEstimate(flops=flops, bytes_accessed=total, transcendentals=0),
        name=name,
    )(*args)


def sds(shape, dtype):
    return jax.ShapeDtypeStruct(shape, dtype)


def plane_kernel(coords, q0, q1, q2, q3, out):
    for k, ref in enumerate((q0, q1, q2, q3)):
        out[pl.ds(pl.multiple_of(((coords[1] + 4 - k) & 3) * 32, 32), 32), :] = ref[...]


def cube_kernel(coords, q0, q1, q2, q3, out, half, rows):
    for k, ref in enumerate((q0, q1, q2, q3)):
        z = ((coords[2] + 4 - k) & 3) * 8
        part = ref[...].astype(F32)
        for i in range(4):
            for j in range(4):
                at = i * 32 + j * 8
                rows[pl.ds(pl.multiple_of(j * E + i * 32 + z, 8), 8), :] = part[at : at + 8]
    out[...] = rows[:, : 3 * E].astype(BF16)
    half[...] = rows[:, 3 * E :].astype(BF16)


def norm_kernel(x_ref, _, o_ref):
    x = x_ref[...].astype(F32)
    mean = jnp.mean(x, axis=-1, keepdims=True)
    cen = x - mean
    inv = lax.rsqrt(jnp.mean(cen * cen, axis=-1, keepdims=True) + EPSILON)
    o_ref[...] = (cen * inv).astype(BF16)


def user_start(pos, meta):
    start = jnp.zeros_like(pos)
    end = 0
    for j in range(3):
        end = end + meta[3, 2 + j]
        start = jnp.where(pos >= end, end, start)
    return start


def places(y, core):
    s = jnp.where(core == 0, 3, 1)
    back, on, far = (y + s) & 3, (y + 4 - s) & 3, (y + 2) & 3
    return (y, back, on, far), (y, on, back, far)


def key_range(base, rows, meta):
    lo = user_start(base, meta)
    last = base + rows - 1
    end = last // R + 1
    first = lo // R
    diag = base // R
    full = jnp.clip((user_start(last, meta) + R - 1) // R, first, diag)
    return first, full, diag, end


def forward_kernel(meta, n0, na, nb, nc, o0, oa, ob, oc, wg, a0, a1, a2, a3, q_s, k_s, v_s):
    y, core = meta[3, 0], meta[3, 1]
    own, oth = places(y, core)
    for blk, ref in zip(own, (n0, na, nb, nc)):
        b = 2 * blk + core
        p = silu(mm(ref[...], wg[:, : 3 * E])).astype(BF16)
        q_s[blk] = p[:, :E]
        k_s[b] = p[:, E : 2 * E]
        v_s[b] = p[:, 2 * E :]
    for blk, ref in zip(oth, (o0, oa, ob, oc)):
        b = 2 * blk + 1 - core
        p = silu(mm(ref[...], wg[:, E : 3 * E])).astype(BF16)
        k_s[b] = p[:, :E]
        v_s[b] = p[:, E:]
    rows = lax.broadcasted_iota(I32, (R, 1), 0)
    lanes = lax.broadcasted_iota(I32, (1, R), 1)
    for k, out in enumerate((a0, a1, a2, a3)):
        blk = (y + k) & 3
        c = 2 * blk + core
        q = q_s[blk]
        pos = rows + c * R
        start = user_start(pos, meta)

        def step(b, acc, masked):
            h = mm(q, k_s[b], NT) * HALF
            w = h + h * jnp.tanh(h)
            if masked:
                key_pos = lanes + b * R
                w = jnp.where((key_pos >= start) & (key_pos <= pos), w, 0.0)
            return acc + mm(w.astype(BF16), v_s[b])

        first, full, diag, end = key_range(c * R, R, meta)
        acc = jnp.zeros((R, E), F32)
        acc = lax.fori_loop(first, full, functools.partial(step, masked=True), acc)
        acc = lax.fori_loop(full, diag, functools.partial(step, masked=False), acc)
        acc = lax.fori_loop(diag, end, functools.partial(step, masked=True), acc)
        mean = jnp.mean(acc, axis=-1, keepdims=True).astype(BF16)
        out[:R] = (acc - mean.astype(F32)).astype(BF16)
        one = (lax.broadcasted_iota(I32, (16, E), 1) == 0).astype(BF16)
        line = mm(one, jnp.broadcast_to(mean, (R, E)), NT)
        out[R:] = jnp.concatenate(
            [line[0:1, i * E : (i + 1) * E] for i in range(4)] + [jnp.zeros((12, E), F32)], axis=0
        ).astype(BF16)


def side_kernel(
    meta, n0, w_mine, wo_half, events, ints, table, bias_w1, bias_w2, u, su, w_out, ev_t, emb, bpre, obs
):
    first = meta[3, 1] == 0
    mine = w_mine[...]
    other = wo_half[...]
    w_u = jnp.where(first, mine, other)
    w_out[...] = jnp.where(first, other, mine)
    act, slope = silu_parts(mm(n0[...], w_u))
    u[...] = act.astype(BF16)
    su[...] = slope.astype(BF16)
    placing = (lax.broadcasted_iota(I32, (R, T), 0) == ints[0:1, :]).astype(BF16)
    ev_t[...] = mm(placing, events[...], TN)
    pid = jnp.broadcast_to(ints[1:2, :], (T, T)).astype(F32).T.astype(I32)
    pid = jnp.concatenate([pid, pid], axis=1)
    selector = (lax.broadcasted_iota(I32, (T, 2 * T), 1) == pid).astype(F32)
    embedded = mm(selector, table[...], precision=HIGHEST)
    bias_pre = mm(embedded, bias_w1[...], precision=HIGHEST)
    emb[...] = embedded
    bpre[...] = bias_pre
    hid = silu(bias_pre)
    obs[...] = jnp.broadcast_to(jnp.sum(hid * bias_w2[...], axis=1, keepdims=True), (T, E))


def slopes_kernel(meta, n0, na, nb, nc, wg, _, s_o, nt, kt):
    y, core = meta[3, 0], meta[3, 1]
    width = s_o.shape[2]
    own, oth = places(y, core)
    for blk, ref in zip(own if width == 3 * E else oth, (n0, na, nb, nc)):
        x = ref[...]
        act, slope = silu_parts(mm(x, wg[:, 3 * E - width : 3 * E]))
        s_o[blk] = slope.astype(BF16)
        kt[blk] = act[:, width - 2 * E : width - E].astype(BF16).T
        nt[blk] = x.T


def middle_kernel(
    meta, r0, r1, r2, r3, u, su, w_out, ev_t, obs, ints, upstream, head_w1, head_w2,
    d0, d1, d2, d3, gated_o, dout_o, dpre_o, picked_o, dhid_o, act_o, drel_o, dobs_o,
    att,
):
    y = meta[3, 0]
    for k, ref in enumerate((r0, r1, r2, r3)):
        h = (y + 4 - k) & 3
        means = ref[R:]
        pick = lax.broadcasted_iota(I32, (16, E), 0)
        column = jnp.concatenate([mm(means, (pick == i).astype(BF16), TN) for i in range(4)], axis=0)
        att[:, pl.ds(pl.multiple_of(h * E, E), E)] = ref[:R].astype(F32) + column
    x = att[...]
    mean = jnp.mean(x, axis=-1, keepdims=True)
    cen = x - mean
    inv = lax.rsqrt(jnp.mean(cen * cen, axis=-1, keepdims=True) + EPSILON)
    normed = cen * inv
    gate = u[...].astype(F32)
    gated = (normed * gate).astype(BF16)
    gated_o[...] = gated
    placing = (lax.broadcasted_iota(I32, (R, T), 0) == ints[0:1, :]).astype(BF16)
    gated_t = mm(placing, gated, TN).astype(BF16)
    picked = (mm(gated_t, w_out[...]) + ev_t[...]).astype(BF16)
    picked_o[...] = picked
    hidden = mm(picked, head_w1[...])
    active, slope = silu_parts(hidden)
    act_o[...] = active
    w2 = head_w2[...]
    relevance = jnp.sum(active * w2, axis=1, keepdims=True)
    observe = obs[:, :1]
    clicked = jnp.broadcast_to(ints[2:3, :], (T, T)).astype(F32).T[:, :1]
    rel_sig = jax.nn.sigmoid(relevance)
    obs_sig = jax.nn.sigmoid(observe)
    missing = jax.nn.sigmoid(-relevance) + rel_sig * jax.nn.sigmoid(-observe)
    d_rel = clicked * (rel_sig - 1.0) + (1.0 - clicked) * rel_sig * (1.0 - rel_sig) * obs_sig / missing
    d_obs = clicked * (obs_sig - 1.0) + (1.0 - clicked) * rel_sig * obs_sig * (1.0 - obs_sig) / missing
    drel_o[...] = jnp.broadcast_to(d_rel, (T, E))
    dobs_o[...] = jnp.broadcast_to(d_obs, (T, E))
    d_hidden = (d_rel * w2 * slope).astype(BF16)
    dhid_o[...] = d_hidden
    d_picked = mm(d_hidden, head_w1[...], NT).astype(BF16)
    d_out = (upstream[...].astype(F32) + mm(placing, d_picked)).astype(BF16)
    dout_o[...] = d_out
    d_gated = mm(d_out, w_out[...], NT)
    dpre_o[...] = (d_gated * normed * su[...].astype(F32)).astype(BF16)
    g = d_gated * gate
    first = jnp.mean(g, axis=-1, keepdims=True)
    second = jnp.mean(g * normed, axis=-1, keepdims=True)
    att[...] = inv * (g - first - normed * second)
    for k, ref in enumerate((d0, d1, d2, d3)):
        h = (y + k) & 3
        ref[...] = att[:, pl.ds(pl.multiple_of(h * E, E), E)].astype(BF16)


def packed(left, right):
    low = (lax.broadcasted_iota(I32, left.shape, 0) & 7) < 4
    n = left.shape[0]
    return jnp.where(low, left, pltpu.roll(right, 4, 0)), jnp.where(low, pltpu.roll(left, n - 4, 0), right)


def grads_kernel(
    meta, n0, dpre, gated, d_out, picked, d_hid, active, d_rel, d_obs, ints, emb, bpre, bias_w1, bias_w2,
    x_own, x_oth, s_own, s_oth,
):
    first = meta[3, 1] == 0

    def put(own_ref, oth_ref, col, left, right):
        x_0, x_1 = packed(left, right)
        cols = slice(col, col + left.shape[1])
        own_ref[:, cols] = jnp.where(first, x_0, x_1).astype(BF16)
        oth_ref[:, cols] = jnp.where(first, x_1, x_0).astype(BF16)

    g_u = mm(n0[...], dpre[...], TN)
    put(x_own, x_oth, 0, g_u[:, :256], g_u[:, 256:])
    g_wo = mm(gated[...], d_out[...], TN)
    put(x_own, x_oth, 256, g_wo[:, :256], g_wo[:, 256:])
    g_h1 = mm(picked[...], d_hid[...], TN)
    put(x_own, x_oth, 512, g_h1[:, :128], g_h1[:, 128:])
    hid, slope = silu_parts(bpre[...])
    d_bias = d_obs[...] * bias_w2[...] * slope
    g_b1 = mm(emb[...], d_bias, TN, HIGHEST)
    d_emb = mm(d_bias, bias_w1[...], NT, HIGHEST)
    pid = jnp.broadcast_to(ints[1:2, :], (2 * T, T))
    select_t = (lax.broadcasted_iota(I32, (2 * T, T), 0) == pid).astype(F32)
    g_tab = mm(select_t, d_emb, precision=HIGHEST)
    h2 = mm(active[...], d_rel[...], TN, HIGHEST)
    b2 = mm(hid, d_obs[...], TN, HIGHEST)
    lane2 = lax.broadcasted_iota(I32, (2 * T, E), 1)
    row2 = lax.broadcasted_iota(I32, (2 * T, E), 0)
    h2 = jnp.where(lane2 == (row2 & 1), h2, 0.0)
    b2 = jnp.where(lax.broadcasted_iota(I32, (T, E), 1) == 2, b2, 0.0)
    o2 = lax.broadcasted_iota(I32, (R, 2 * T), 0)
    i2 = lax.broadcasted_iota(I32, (R, 2 * T), 1)
    o1 = lax.broadcasted_iota(I32, (R, T), 0)
    i1 = lax.broadcasted_iota(I32, (R, T), 1)
    parts = []
    for cc in range(2):
        dest2 = 2 * (o2 >> 3) + cc
        dest1 = 2 * (o1 >> 3) + cc
        p_tab = (((o2 & 7) == 4) & (i2 == 2 * dest2)) | (((o2 & 7) == 5) & (i2 == 2 * dest2 + 1))
        p_h2 = ((o2 & 7) == 7) & ((i2 >> 1) == dest2)
        p_b1 = ((o1 & 7) == 6) & (i1 == dest1)
        p_b2 = ((o1 & 7) == 7) & (i1 == dest1)
        parts.append(
            mm(p_tab.astype(BF16), g_tab.astype(BF16))
            + mm(p_h2.astype(BF16), h2.astype(BF16))
            + mm(p_b1.astype(BF16), g_b1.astype(BF16))
            + mm(p_b2.astype(BF16), b2.astype(BF16))
        )
    s_own[...] = jnp.where(first, parts[0], parts[1]).astype(BF16)
    s_oth[...] = jnp.where(first, parts[1], parts[0]).astype(BF16)


def backward_kernel(
    meta, q_s, k_s, v_s, r0, r1, r2, r3, s_a, s_b, nt_a, nt_b, kt_a, kt_b, s_own, s_oth,
    x_own, x_oth,
    dq_s, dk_s, dv_s, kt_s,
):
    y, core = meta[3, 0], meta[3, 1]
    for i in range(4):
        kt_s[2 * i + core] = kt_a[i]
        kt_s[2 * i + 1 - core] = kt_b[i]
    dk_s[...] = jnp.zeros_like(dk_s)
    dv_s[...] = jnp.zeros_like(dv_s)
    rows = lax.broadcasted_iota(I32, (R, 1), 0)
    lanes = lax.broadcasted_iota(I32, (1, R), 1)
    for k, ref in enumerate((r0, r1, r2, r3)):
        blk = (y + 4 - k) & 3
        c = 2 * blk + core
        q = q_s[blk]
        g = ref[...]
        pos = lanes + c * R
        start = user_start(pos, meta)

        def step(b, dq, masked):
            kb = k_s[b]
            h = mm(kb, q, NT) * HALF
            dp = mm(v_s[b], g, NT)
            t = jnp.tanh(h)
            a = 1.0 + t
            w = h * a
            d = dp * (a + w * (1.0 - t))
            if masked:
                key_pos = rows + b * R
                keep = (key_pos >= start) & (key_pos <= pos)
                w = jnp.where(keep, w, 0.0)
                d = jnp.where(keep, d, 0.0)
            w = w.astype(BF16)
            d = d.astype(BF16)
            dv_s[b] += mm(w, g)
            dk_s[b] += mm(d, q)
            return dq + mm(kt_s[b], d)

        first, full, diag, end = key_range(c * R, R, meta)
        acc = jnp.zeros((E, R), F32)
        acc = lax.fori_loop(first, full, functools.partial(step, masked=True), acc)
        acc = lax.fori_loop(full, diag, functools.partial(step, masked=False), acc)
        acc = lax.fori_loop(diag, end, functools.partial(step, masked=True), acc)
        dq_s[blk] = acc.T
    g_all = jnp.zeros((W, 3 * E), F32)
    g_kv = jnp.zeros((W, 2 * E), F32)
    for i in range(4):
        b = 2 * i + core
        d = jnp.concatenate([dq_s[i] * HALF, dk_s[b] * HALF, dv_s[b]], axis=1) * s_a[i].astype(F32)
        g_all = g_all + mm(nt_a[i], d.astype(BF16))
        b = 2 * i + 1 - core
        d = jnp.concatenate([dk_s[b] * HALF, dv_s[b]], axis=1) * s_b[i].astype(F32)
        g_kv = g_kv + mm(nt_b[i], d.astype(BF16))
    g_q = g_all[:, :E]
    g_k = g_all[:, E : 2 * E] + g_kv[:, :E]
    g_v = g_all[:, 2 * E :] + g_kv[:, E:]
    first = core == 0
    low = (lax.broadcasted_iota(I32, (W, E), 0) & 7) < 4
    x_0, x_1 = packed(g_q, g_k)
    x_own[:, :E] = jnp.where(first, x_0, x_1).astype(BF16)
    x_oth[:, :E] = jnp.where(first, x_1, x_0).astype(BF16)
    v_1 = pltpu.roll(g_v, W - 4, 0)
    x_own[:, E:] = jnp.where(low, jnp.where(first, g_v, v_1), s_own[...].astype(F32)).astype(BF16)
    x_oth[:, E:] = jnp.where(low, jnp.where(first, v_1, g_v), s_oth[...].astype(F32)).astype(BF16)


def sum_kernel(x_ref, g_in, g_out, g_h1, g_small):
    total = None
    for h in range(HEADS):
        part = jnp.zeros((8, 7 * E), F32)
        for i in range(16):
            at = (h * 16 + i) * 8
            part = part + x_ref[at : at + 8, :].astype(F32)
        g_in[:, W + h * E : W + (h + 1) * E] = part[0:4, 6 * E :]
        g_in[:, 2 * W + h * E : 2 * W + (h + 1) * E] = part[0:4, 5 * E : 6 * E]
        g_in[:, 3 * W + h * E : 3 * W + (h + 1) * E] = part[4:8, 5 * E : 6 * E]
        total = part if total is None else total + part
    g_in[:, 0:256] = total[0:4, 0:256]
    g_in[:, 256:512] = total[4:8, 0:256]
    g_out[:, 0:256] = total[0:4, 256:512]
    g_out[:, 256:512] = total[4:8, 256:512]
    g_h1[:, 0:128] = total[0:4, 512:640]
    g_h1[:, 128:256] = total[4:8, 512:640]
    g_small[...] = total[4:8, 768:896]


CHIPS = ("y", "xh", "xl", "z")
SWAP = []
for _i in range(32):
    _xh, _rest, _core = _i // 16, (_i // 2) % 8, _i % 2
    SWAP.append((_i, _i if _xh == _core else (1 - _xh) * 16 + _rest * 2 + 1 - _core))


def swapped(x):
    return lax.ppermute(x, ("xh", "xl", "z", "core"), SWAP)


def across(x):
    return lax.ppermute(x, "core", [(0, 1), (1, 0)])


def ring(x, k):
    return lax.ppermute(x, "y", [(i, (i + k) % 4) for i in range(4)])


def moved(x, axes, k):
    return lax.ppermute(x, axes, [(i, (i + k) % 4) for i in range(4)])


def tie(x, other):
    space = pl.BlockSpec(memory_space=pltpu.VMEM)
    return pl.pallas_call(
        lambda *_: None,
        out_shape=sds(x.shape, x.dtype),
        in_specs=[space] * 2,
        out_specs=space,
        compiler_params=pltpu.CompilerParams(vmem_limit_bytes=4 << 20),
        input_output_aliases={0: 0},
        name="tie",
    )(x, other)


def turned(x, k):
    return lax.ppermute(
        x, ("y", "core"), [(2 * i + c, 2 * ((i + (k if c == 0 else -k)) % 4) + c) for i in range(4) for c in range(2)]
    )


def body(
    events, lengths, target_rows, position_ids, labels, upstream,
    w_in, w_out, head_w1, head_w2, table, bias_w1, bias_w2,
):
    y, core = lax.axis_index("y"), lax.axis_index("core")
    w_rows = jnp.concatenate([w_in, w_out], axis=1)
    w_other = across(w_rows)
    w_rows = jnp.where(
        core == 0, jnp.concatenate([w_rows, w_other], axis=0), jnp.concatenate([w_other, w_rows], axis=0)
    )
    shared = jnp.where(core == 0, w_rows[:, :W], w_rows[:, 4 * W :])
    w_rows = jnp.concatenate([w_rows[:, W : 4 * W], shared], axis=1)
    x, z = 2 * lax.axis_index("xh") + lax.axis_index("xl"), lax.axis_index("z")
    line = [moved(w_rows, ("y",), k) for k in (3, 2, 1)]
    line = jnp.concatenate(line + [w_rows] + line, axis=0)
    line = lax.dynamic_slice_in_dim(line, ((3 - y) & 3) * 8, 32, 0)
    line = jnp.concatenate(
        [lax.dynamic_slice_in_dim(line, at + y * E, E, 1) for at in (W, 2 * W, 0)] + [line[:, 3 * W :]], axis=1
    )
    coords = jnp.stack([y, x, z]).astype(I32)
    (plane,) = call(
        plane_kernel,
        [sds((E, 7 * E), BF16)],
        [coords, line] + [moved(line, ("xh", "xl"), k) for k in (1, 2, 3)],
        limit=8,
        name="plane",
    )
    wg, w_mine = call(
        cube_kernel,
        [sds((W, 3 * E), BF16), sds((W, W), BF16)],
        [coords, plane] + [moved(plane, ("z",), k) for k in (1, 2, 3)],
        scratch=[pltpu.VMEM((W, 7 * E), F32)],
        limit=12,
        name="cube",
    )

    w_half = across(w_mine)

    ev = swapped(events[0])
    place = jnp.stack([y, lax.axis_index("xh")]).astype(I32)[None]
    line = jnp.pad(jnp.concatenate([place, lengths], axis=1), ((0, 0), (0, T - 6)))
    ints = swapped(jnp.concatenate([target_rows, position_ids, labels, line], axis=0))
    meta = ints
    (n0,) = call(norm_kernel, [sds((R, W), BF16)], [ev, line], n_smem=0, n_any=1, limit=12, name="norm")
    na = turned(n0, 1)
    nb = turned(n0, 3)
    na = tie(na, plane)
    nc = turned(na, 1)
    n0, nb, na = tie(n0, wg), tie(nb, wg), tie(na, nc)
    parts = [n0, na, nb, nc]
    parts = parts + [across(p) for p in parts]
    up = swapped(upstream[0])

    qkv = [sds((4, R, E), BF16), sds((8, R, E), BF16), sds((8, R, E), BF16)]
    a0, a1, a2, a3, q_s, k_s, v_s = call(
        forward_kernel, [sds((R + 16, E), BF16)] * 4 + qkv, [meta] + parts + [wg], flops=5 * 10**9, name="forward"
    )
    r2, r1, r3 = ring(a2, 2), ring(a1, 1), ring(a3, 3)
    u, su, w_o, ev_t, emb, bpre, obs = call(
        side_kernel,
        [sds((R, W), BF16)] * 3 + [sds((T, W), F32)] + [sds((T, E), F32)] * 3,
        [meta, n0, w_mine, w_half, ev, ints, table, bias_w1, bias_w2.reshape(1, E)],
        flops=10**9,
        name="side",
    )

    def slopes(width, blocks, after):
        return call(
            slopes_kernel,
            [sds((4, R, width), BF16), sds((4, W, R), BF16), sds((4, E, R), BF16)],
            [meta] + blocks + [wg, after],
            n_any=1,
            flops=10**9,
            name="slopes",
        )

    s_a, nt_a, kt_a = slopes(3 * E, parts[:4], a0)
    w2 = head_w2.reshape(1, 2 * E)
    b2 = bias_w2.reshape(1, E)
    d0, d1, d2, d3, gated, d_out, dpre, picked, d_hid, active, d_rel, d_obs = call(
        middle_kernel,
        [sds((R, E), BF16)] * 4
        + [sds((R, W), BF16)] * 3
        + [sds((T, W), BF16), sds((T, 2 * E), BF16), sds((T, 2 * E), F32), sds((T, E), F32), sds((T, E), F32)],
        [meta, a0, r1, r2, r3, u, su, w_o, ev_t, obs, ints, up, head_w1, w2],
        scratch=[pltpu.VMEM((R, W), F32)],
        flops=10**9,
        name="middle",
    )
    g2, g1, g3 = ring(d2, 2), ring(d1, 1), ring(d3, 3)
    s_b, nt_b, kt_b = slopes(2 * E, parts[4:], d0)
    early, early_oth, s_own, s_oth = call(
        grads_kernel,
        [sds((R, 5 * E), BF16)] * 2 + [sds((R, E), BF16)] * 2,
        [meta, n0, dpre, gated, d_out, picked, d_hid, active, d_rel, d_obs, ints, emb, bpre, bias_w1, b2],
        flops=2 * 10**9,
        name="grads",
    )
    early_in = across(early_oth)
    late, late_oth = call(
        backward_kernel,
        [sds((R, 2 * E), BF16)] * 2,
        [meta, q_s, k_s, v_s, d0, g1, g2, g3, s_a, s_b, nt_a, nt_b, kt_a, kt_b, s_own, s_oth],
        scratch=[pltpu.VMEM((4, R, E), F32), pltpu.VMEM((8, R, E), F32), pltpu.VMEM((8, R, E), F32)]
        + [pltpu.VMEM((8, E, R), BF16)],
        flops=10**10,
        limit=28,
        name="backward",
    )
    late_in = across(late_oth)
    pair = jnp.concatenate(
        [
            (early.astype(F32) + early_in.astype(F32)).astype(BF16),
            (late.astype(F32) + late_in.astype(F32)).astype(BF16),
        ],
        axis=1,
    )
    got = lax.all_to_all(pair, CHIPS, 0, 0, tiled=True)
    g_in, g_out, g_h1, g_small = call(
        sum_kernel,
        [sds((4, 4 * W), F32), sds((4, W), F32), sds((4, 2 * E), F32), sds((4, E), F32)],
        [got],
        n_smem=0,
        name="total",
    )
    return g_in, g_out, g_h1, g_small[3, 0:2], g_small[0:2], g_small[2:3], g_small[3, 2:3]


def solution(mesh):
    fine = Mesh(mesh.devices.reshape(4, 2, 2, 4, 2), ("y", "xh", "xl", "z", "core"))
    ctx, dp = ("y", "xh"), ("xl", "z", "core")
    every = ctx + dp
    in_specs = (
        P(dp, ctx, None),
        P(dp, None),
        P(dp, ctx),
        P(dp, ctx),
        P(dp, ctx),
        P(dp, ctx, None),
        P(every, None),
        P(every, None),
        P(),
        P(),
        P(),
        P(),
        P(),
    )
    out_specs = (
        P(every, None),
        P(every, None),
        P(every, None),
        P(every),
        P(every, None),
        P(every, None),
        P(every),
    )
    return jax.shard_map(body, mesh=fine, in_specs=in_specs, out_specs=out_specs, check_vma=False)
```

```python
import functools
import math

import jax
import jax.numpy as jnp
from jax import lax
from jax.experimental import pallas as pl
from jax.experimental.pallas import tpu as pltpu
from jax.sharding import Mesh, PartitionSpec as P

HEADS = 4
EPSILON = 1e-05
HIGHEST = lax.Precision.HIGHEST
F32 = jnp.float32
BF16 = jnp.bfloat16
I32 = jnp.int32
R = 512
W = 512
E = 128
T = 128
SCALE = 1.0 / math.sqrt(E)
HALF = 0.5 * SCALE

NN = (((1,), (0,)), ((), ()))
NT = (((1,), (1,)), ((), ()))
TN = (((0,), (0,)), ((), ()))


def mm(a, b, dims=NN, precision=None):
    return lax.dot_general(a, b, dims, precision=precision, preferred_element_type=F32)


def silu_parts(z):
    h = 0.5 * z
    t = jnp.tanh(h)
    a = 1.0 + t
    w = h * a
    return w, 0.5 * (a + w * (1.0 - t))


def silu(z):
    h = 0.5 * z
    return h + h * jnp.tanh(h)


def vmem(n):
    return [pl.BlockSpec(memory_space=pltpu.VMEM)] * n


def smem():
    return [pl.BlockSpec(memory_space=pltpu.SMEM)]


def call(kernel, outs, args, scratch=(), limit=24, flops=0, n_smem=1, n_any=0, name=None):
    total = sum(a.size * a.dtype.itemsize for a in args) + sum(
        math.prod(o.shape) * o.dtype.itemsize for o in outs
    )
    return pl.pallas_call(
        kernel,
        out_shape=tuple(outs),
        in_specs=smem() * n_smem
        + vmem(len(args) - n_smem - n_any)
        + [pl.BlockSpec(memory_space=pl.ANY)] * n_any,
        out_specs=tuple(vmem(len(outs))),
        scratch_shapes=list(scratch),
        compiler_params=pltpu.CompilerParams(vmem_limit_bytes=limit << 20),
        cost_estimate=pl.CostEstimate(flops=flops, bytes_accessed=total, transcendentals=0),
        name=name,
    )(*args)


def sds(shape, dtype):
    return jax.ShapeDtypeStruct(shape, dtype)


def plane_kernel(coords, q0, q1, q2, q3, out):
    for k, ref in enumerate((q0, q1, q2, q3)):
        out[pl.ds(pl.multiple_of(((coords[1] + 4 - k) & 3) * 32, 32), 32), :] = ref[...]


def cube_kernel(coords, q0, q1, q2, q3, out, half, rows):
    for k, ref in enumerate((q0, q1, q2, q3)):
        z = ((coords[2] + 4 - k) & 3) * 8
        part = ref[...].astype(F32)
        for i in range(4):
            for j in range(4):
                at = i * 32 + j * 8
                rows[pl.ds(pl.multiple_of(j * E + i * 32 + z, 8), 8), :] = part[at : at + 8]
    out[...] = rows[:, : 3 * E].astype(BF16)
    half[...] = rows[:, 3 * E :].astype(BF16)


def norm_kernel(x_ref, _, o_ref):
    x = x_ref[...].astype(F32)
    mean = jnp.mean(x, axis=-1, keepdims=True)
    cen = x - mean
    inv = lax.rsqrt(jnp.mean(cen * cen, axis=-1, keepdims=True) + EPSILON)
    o_ref[...] = (cen * inv).astype(BF16)


def user_start(pos, meta):
    start = jnp.zeros_like(pos)
    end = 0
    for j in range(3):
        end = end + meta[3, 2 + j]
        start = jnp.where(pos >= end, end, start)
    return start


def places(y, core):
    s = jnp.where(core == 0, 3, 1)
    back, on, far = (y + s) & 3, (y + 4 - s) & 3, (y + 2) & 3
    return (y, back, on, far), (y, on, back, far)


def key_range(base, rows, meta):
    lo = user_start(base, meta)
    last = base + rows - 1
    end = last // R + 1
    first = lo // R
    diag = base // R
    full = jnp.clip((user_start(last, meta) + R - 1) // R, first, diag)
    return first, full, diag, end


def forward_kernel(meta, n0, na, nb, nc, o0, oa, ob, oc, wg, a0, a1, a2, a3, q_s, k_s, v_s, sent):
    y, core = meta[3, 0], meta[3, 1]
    own, oth = places(y, core)
    for blk, ref in zip(own, (n0, na, nb, nc)):
        b = 2 * blk + core
        p = silu(mm(ref[...], wg[:, : 3 * E])).astype(BF16)
        q_s[blk] = p[:, :E]
        k_s[b] = p[:, E : 2 * E]
        v_s[b] = p[:, 2 * E :]
    for blk, ref in zip(oth, (o0, oa, ob, oc)):
        b = 2 * blk + 1 - core
        p = silu(mm(ref[...], wg[:, E : 3 * E])).astype(BF16)
        k_s[b] = p[:, :E]
        v_s[b] = p[:, E:]
    rows = lax.broadcasted_iota(I32, (R, 1), 0)
    lanes = lax.broadcasted_iota(I32, (1, R), 1)

    def block(k, _):
        blk = (y + k) & 3
        c = 2 * blk + core
        q = q_s[blk]
        pos = rows + c * R
        start = user_start(pos, meta)

        def step(b, acc, masked):
            h = mm(q, k_s[b], NT) * HALF
            w = h + h * jnp.tanh(h)
            if masked:
                key_pos = lanes + b * R
                w = jnp.where((key_pos >= start) & (key_pos <= pos), w, 0.0)
            return acc + mm(w.astype(BF16), v_s[b])

        first, full, diag, end = key_range(c * R, R, meta)
        acc = jnp.zeros((R, E), F32)
        acc = lax.fori_loop(first, full, functools.partial(step, masked=True), acc)
        acc = lax.fori_loop(full, diag, functools.partial(step, masked=False), acc)
        acc = lax.fori_loop(diag, end, functools.partial(step, masked=True), acc)
        mean = jnp.mean(acc, axis=-1, keepdims=True).astype(BF16)
        sent[k, :R] = (acc - mean.astype(F32)).astype(BF16)
        one = (lax.broadcasted_iota(I32, (16, E), 1) == 0).astype(BF16)
        line = mm(one, jnp.broadcast_to(mean, (R, E)), NT)
        sent[k, R:] = jnp.concatenate(
            [line[0:1, i * E : (i + 1) * E] for i in range(4)] + [jnp.zeros((12, E), F32)], axis=0
        ).astype(BF16)
        return 0

    lax.fori_loop(0, 4, block, 0)
    for k, out in enumerate((a0, a1, a2, a3)):
        out[...] = sent[k]


def side_kernel(
    meta, n0, w_mine, wo_half, events, ints, table, bias_w1, bias_w2, u, su, w_out, ev_t, emb, bpre, obs
):
    first = meta[3, 1] == 0
    mine = w_mine[...]
    other = wo_half[...]
    w_u = jnp.where(first, mine, other)
    w_out[...] = jnp.where(first, other, mine)
    act, slope = silu_parts(mm(n0[...], w_u))
    u[...] = act.astype(BF16)
    su[...] = slope.astype(BF16)
    placing = (lax.broadcasted_iota(I32, (R, T), 0) == ints[0:1, :]).astype(BF16)
    ev_t[...] = mm(placing, events[...], TN)
    pid = jnp.broadcast_to(ints[1:2, :], (T, T)).astype(F32).T.astype(I32)
    pid = jnp.concatenate([pid, pid], axis=1)
    selector = (lax.broadcasted_iota(I32, (T, 2 * T), 1) == pid).astype(F32)
    embedded = mm(selector, table[...], precision=HIGHEST)
    bias_pre = mm(embedded, bias_w1[...], precision=HIGHEST)
    emb[...] = embedded
    bpre[...] = bias_pre
    hid = silu(bias_pre)
    obs[...] = jnp.broadcast_to(jnp.sum(hid * bias_w2[...], axis=1, keepdims=True), (T, E))


def slopes_kernel(meta, n0, na, nb, nc, wg, _, s_o, nt, kt):
    y, core = meta[3, 0], meta[3, 1]
    width = s_o.shape[2]
    own, oth = places(y, core)
    for blk, ref in zip(own if width == 3 * E else oth, (n0, na, nb, nc)):
        x = ref[...]
        act, slope = silu_parts(mm(x, wg[:, 3 * E - width : 3 * E]))
        s_o[blk] = slope.astype(BF16)
        kt[blk] = act[:, width - 2 * E : width - E].astype(BF16).T
        nt[blk] = x.T


def middle_kernel(
    meta, r0, r1, r2, r3, u, su, w_out, ev_t, obs, ints, upstream, head_w1, head_w2,
    d0, d1, d2, d3, gated_o, dout_o, dpre_o, picked_o, dhid_o, act_o, drel_o, dobs_o,
    att,
):
    y = meta[3, 0]
    for k, ref in enumerate((r0, r1, r2, r3)):
        h = (y + 4 - k) & 3
        means = ref[R:]
        pick = lax.broadcasted_iota(I32, (16, E), 0)
        column = jnp.concatenate([mm(means, (pick == i).astype(BF16), TN) for i in range(4)], axis=0)
        att[:, pl.ds(pl.multiple_of(h * E, E), E)] = ref[:R].astype(F32) + column
    x = att[...]
    mean = jnp.mean(x, axis=-1, keepdims=True)
    cen = x - mean
    inv = lax.rsqrt(jnp.mean(cen * cen, axis=-1, keepdims=True) + EPSILON)
    normed = cen * inv
    gate = u[...].astype(F32)
    gated = (normed * gate).astype(BF16)
    gated_o[...] = gated
    placing = (lax.broadcasted_iota(I32, (R, T), 0) == ints[0:1, :]).astype(BF16)
    gated_t = mm(placing, gated, TN).astype(BF16)
    picked = (mm(gated_t, w_out[...]) + ev_t[...]).astype(BF16)
    picked_o[...] = picked
    hidden = mm(picked, head_w1[...])
    active, slope = silu_parts(hidden)
    act_o[...] = active
    w2 = head_w2[...]
    relevance = jnp.sum(active * w2, axis=1, keepdims=True)
    observe = obs[:, :1]
    clicked = jnp.broadcast_to(ints[2:3, :], (T, T)).astype(F32).T[:, :1]
    rel_sig = jax.nn.sigmoid(relevance)
    obs_sig = jax.nn.sigmoid(observe)
    missing = jax.nn.sigmoid(-relevance) + rel_sig * jax.nn.sigmoid(-observe)
    d_rel = clicked * (rel_sig - 1.0) + (1.0 - clicked) * rel_sig * (1.0 - rel_sig) * obs_sig / missing
    d_obs = clicked * (obs_sig - 1.0) + (1.0 - clicked) * rel_sig * obs_sig * (1.0 - obs_sig) / missing
    drel_o[...] = jnp.broadcast_to(d_rel, (T, E))
    dobs_o[...] = jnp.broadcast_to(d_obs, (T, E))
    d_hidden = (d_rel * w2 * slope).astype(BF16)
    dhid_o[...] = d_hidden
    d_picked = mm(d_hidden, head_w1[...], NT).astype(BF16)
    d_out = (upstream[...].astype(F32) + mm(placing, d_picked)).astype(BF16)
    dout_o[...] = d_out
    d_gated = mm(d_out, w_out[...], NT)
    dpre_o[...] = (d_gated * normed * su[...].astype(F32)).astype(BF16)
    g = d_gated * gate
    first = jnp.mean(g, axis=-1, keepdims=True)
    second = jnp.mean(g * normed, axis=-1, keepdims=True)
    att[...] = inv * (g - first - normed * second)
    for k, ref in enumerate((d0, d1, d2, d3)):
        h = (y + k) & 3
        ref[...] = att[:, pl.ds(pl.multiple_of(h * E, E), E)].astype(BF16)


def packed(left, right):
    low = (lax.broadcasted_iota(I32, left.shape, 0) & 7) < 4
    n = left.shape[0]
    return jnp.where(low, left, pltpu.roll(right, 4, 0)), jnp.where(low, pltpu.roll(left, n - 4, 0), right)


def grads_kernel(
    meta, n0, dpre, gated, d_out, picked, d_hid, active, d_rel, d_obs, ints, emb, bpre, bias_w1, bias_w2,
    x_own, x_oth, s_own, s_oth,
):
    first = meta[3, 1] == 0

    def put(own_ref, oth_ref, col, left, right):
        x_0, x_1 = packed(left, right)
        cols = slice(col, col + left.shape[1])
        own_ref[:, cols] = jnp.where(first, x_0, x_1).astype(BF16)
        oth_ref[:, cols] = jnp.where(first, x_1, x_0).astype(BF16)

    g_u = mm(n0[...], dpre[...], TN)
    put(x_own, x_oth, 0, g_u[:, :256], g_u[:, 256:])
    g_wo = mm(gated[...], d_out[...], TN)
    put(x_own, x_oth, 256, g_wo[:, :256], g_wo[:, 256:])
    g_h1 = mm(picked[...], d_hid[...], TN)
    put(x_own, x_oth, 512, g_h1[:, :128], g_h1[:, 128:])
    hid, slope = silu_parts(bpre[...])
    d_bias = d_obs[...] * bias_w2[...] * slope
    g_b1 = mm(emb[...], d_bias, TN, HIGHEST)
    d_emb = mm(d_bias, bias_w1[...], NT, HIGHEST)
    pid = jnp.broadcast_to(ints[1:2, :], (2 * T, T))
    select_t = (lax.broadcasted_iota(I32, (2 * T, T), 0) == pid).astype(F32)
    g_tab = mm(select_t, d_emb, precision=HIGHEST)
    h2 = mm(active[...], d_rel[...], TN, HIGHEST)
    b2 = mm(hid, d_obs[...], TN, HIGHEST)
    lane2 = lax.broadcasted_iota(I32, (2 * T, E), 1)
    row2 = lax.broadcasted_iota(I32, (2 * T, E), 0)
    h2 = jnp.where(lane2 == (row2 & 1), h2, 0.0)
    b2 = jnp.where(lax.broadcasted_iota(I32, (T, E), 1) == 2, b2, 0.0)
    o2 = lax.broadcasted_iota(I32, (R, 2 * T), 0)
    i2 = lax.broadcasted_iota(I32, (R, 2 * T), 1)
    o1 = lax.broadcasted_iota(I32, (R, T), 0)
    i1 = lax.broadcasted_iota(I32, (R, T), 1)
    parts = []
    for cc in range(2):
        dest2 = 2 * (o2 >> 3) + cc
        dest1 = 2 * (o1 >> 3) + cc
        p_tab = (((o2 & 7) == 4) & (i2 == 2 * dest2)) | (((o2 & 7) == 5) & (i2 == 2 * dest2 + 1))
        p_h2 = ((o2 & 7) == 7) & ((i2 >> 1) == dest2)
        p_b1 = ((o1 & 7) == 6) & (i1 == dest1)
        p_b2 = ((o1 & 7) == 7) & (i1 == dest1)
        parts.append(
            mm(p_tab.astype(BF16), g_tab.astype(BF16))
            + mm(p_h2.astype(BF16), h2.astype(BF16))
            + mm(p_b1.astype(BF16), g_b1.astype(BF16))
            + mm(p_b2.astype(BF16), b2.astype(BF16))
        )
    s_own[...] = jnp.where(first, parts[0], parts[1]).astype(BF16)
    s_oth[...] = jnp.where(first, parts[1], parts[0]).astype(BF16)


def backward_kernel(
    meta, q_s, k_s, v_s, r0, r1, r2, r3, s_a, s_b, nt_a, nt_b, kt_a, kt_b, s_own, s_oth,
    x_own, x_oth,
    dq_s, dk_s, dv_s, kt_s, g_s,
):
    y, core = meta[3, 0], meta[3, 1]
    for i in range(4):
        kt_s[2 * i + core] = kt_a[i]
        kt_s[2 * i + 1 - core] = kt_b[i]
    dk_s[...] = jnp.zeros_like(dk_s)
    dv_s[...] = jnp.zeros_like(dv_s)
    rows = lax.broadcasted_iota(I32, (R, 1), 0)
    lanes = lax.broadcasted_iota(I32, (1, R), 1)
    for k, ref in enumerate((r0, r1, r2, r3)):
        g_s[(y + 4 - k) & 3] = ref[...]

    def block(blk, _):
        c = 2 * blk + core
        q = q_s[blk]
        g = g_s[blk]
        pos = lanes + c * R
        start = user_start(pos, meta)

        def step(b, dq, masked):
            kb = k_s[b]
            h = mm(kb, q, NT) * HALF
            dp = mm(v_s[b], g, NT)
            t = jnp.tanh(h)
            a = 1.0 + t
            w = h * a
            d = dp * (a + w * (1.0 - t))
            if masked:
                key_pos = rows + b * R
                keep = (key_pos >= start) & (key_pos <= pos)
                w = jnp.where(keep, w, 0.0)
                d = jnp.where(keep, d, 0.0)
            w = w.astype(BF16)
            d = d.astype(BF16)
            dv_s[b] += mm(w, g)
            dk_s[b] += mm(d, q)
            return dq + mm(kt_s[b], d)

        first, full, diag, end = key_range(c * R, R, meta)
        acc = jnp.zeros((E, R), F32)
        acc = lax.fori_loop(first, full, functools.partial(step, masked=True), acc)
        acc = lax.fori_loop(full, diag, functools.partial(step, masked=False), acc)
        acc = lax.fori_loop(diag, end, functools.partial(step, masked=True), acc)
        dq_s[blk] = acc.T
        return 0

    lax.fori_loop(0, 4, block, 0)
    g_all = jnp.zeros((W, 3 * E), F32)
    g_kv = jnp.zeros((W, 2 * E), F32)
    for i in range(4):
        b = 2 * i + core
        d = jnp.concatenate([dq_s[i] * HALF, dk_s[b] * HALF, dv_s[b]], axis=1) * s_a[i].astype(F32)
        g_all = g_all + mm(nt_a[i], d.astype(BF16))
        b = 2 * i + 1 - core
        d = jnp.concatenate([dk_s[b] * HALF, dv_s[b]], axis=1) * s_b[i].astype(F32)
        g_kv = g_kv + mm(nt_b[i], d.astype(BF16))
    g_q = g_all[:, :E]
    g_k = g_all[:, E : 2 * E] + g_kv[:, :E]
    g_v = g_all[:, 2 * E :] + g_kv[:, E:]
    first = core == 0
    low = (lax.broadcasted_iota(I32, (W, E), 0) & 7) < 4
    x_0, x_1 = packed(g_q, g_k)
    x_own[:, :E] = jnp.where(first, x_0, x_1).astype(BF16)
    x_oth[:, :E] = jnp.where(first, x_1, x_0).astype(BF16)
    v_1 = pltpu.roll(g_v, W - 4, 0)
    x_own[:, E:] = jnp.where(low, jnp.where(first, g_v, v_1), s_own[...].astype(F32)).astype(BF16)
    x_oth[:, E:] = jnp.where(low, jnp.where(first, v_1, g_v), s_oth[...].astype(F32)).astype(BF16)


def sum_kernel(x_ref, g_in, g_out, g_h1, g_h2, g_tab, g_b1, g_b2):
    total = None
    for h in range(HEADS):
        part = jnp.zeros((8, 7 * E), F32)
        for i in range(16):
            at = (h * 16 + i) * 8
            part = part + x_ref[at : at + 8, :].astype(F32)
        g_in[:, W + h * E : W + (h + 1) * E] = part[0:4, 6 * E :]
        g_in[:, 2 * W + h * E : 2 * W + (h + 1) * E] = part[0:4, 5 * E : 6 * E]
        g_in[:, 3 * W + h * E : 3 * W + (h + 1) * E] = part[4:8, 5 * E : 6 * E]
        total = part if total is None else total + part
    g_in[:, 0:256] = total[0:4, 0:256]
    g_in[:, 256:512] = total[4:8, 0:256]
    g_out[:, 0:256] = total[0:4, 256:512]
    g_out[:, 256:512] = total[4:8, 256:512]
    g_h1[:, 0:128] = total[0:4, 512:640]
    g_h1[:, 128:256] = total[4:8, 512:640]
    g_tab[...] = total[4:6, 768:896]
    g_b1[...] = total[6:7, 768:896]
    g_h2[...] = total[7:8, 768:770]
    g_b2[...] = total[7:8, 770:771]


CHIPS = ("y", "xh", "xl", "z")
SWAP = []
for _i in range(32):
    _xh, _rest, _core = _i // 16, (_i // 2) % 8, _i % 2
    SWAP.append((_i, _i if _xh == _core else (1 - _xh) * 16 + _rest * 2 + 1 - _core))


def swapped(x):
    return lax.ppermute(x, ("xh", "xl", "z", "core"), SWAP)


def across(x):
    return lax.ppermute(x, "core", [(0, 1), (1, 0)])


def ring(x, k):
    return lax.ppermute(x, "y", [(i, (i + k) % 4) for i in range(4)])


def moved(x, axes, k):
    return lax.ppermute(x, axes, [(i, (i + k) % 4) for i in range(4)])


def tie(x, other):
    space = pl.BlockSpec(memory_space=pltpu.VMEM)
    return pl.pallas_call(
        lambda *_: None,
        out_shape=sds(x.shape, x.dtype),
        in_specs=[space] * 2,
        out_specs=space,
        compiler_params=pltpu.CompilerParams(vmem_limit_bytes=4 << 20),
        input_output_aliases={0: 0},
        name="tie",
    )(x, other)


def turned(x, k):
    return lax.ppermute(
        x, ("y", "core"), [(2 * i + c, 2 * ((i + (k if c == 0 else -k)) % 4) + c) for i in range(4) for c in range(2)]
    )


def body(
    events, lengths, target_rows, position_ids, labels, upstream,
    w_in, w_out, head_w1, head_w2, table, bias_w1, bias_w2,
):
    y, core = lax.axis_index("y"), lax.axis_index("core")
    w_rows = jnp.concatenate([w_in, w_out], axis=1)
    w_other = across(w_rows)
    w_rows = jnp.where(
        core == 0, jnp.concatenate([w_rows, w_other], axis=0), jnp.concatenate([w_other, w_rows], axis=0)
    )
    shared = jnp.where(core == 0, w_rows[:, :W], w_rows[:, 4 * W :])
    w_rows = jnp.concatenate([w_rows[:, W : 4 * W], shared], axis=1)
    x, z = 2 * lax.axis_index("xh") + lax.axis_index("xl"), lax.axis_index("z")
    line = [moved(w_rows, ("y",), k) for k in (3, 2, 1)]
    line = jnp.concatenate(line + [w_rows] + line, axis=0)
    line = lax.dynamic_slice_in_dim(line, ((3 - y) & 3) * 8, 32, 0)
    line = jnp.concatenate(
        [lax.dynamic_slice_in_dim(line, at + y * E, E, 1) for at in (W, 2 * W, 0)] + [line[:, 3 * W :]], axis=1
    )
    coords = jnp.stack([y, x, z]).astype(I32)
    (plane,) = call(
        plane_kernel,
        [sds((E, 7 * E), BF16)],
        [coords, line] + [moved(line, ("xh", "xl"), k) for k in (1, 2, 3)],
        limit=8,
        name="plane",
    )
    wg, w_mine = call(
        cube_kernel,
        [sds((W, 3 * E), BF16), sds((W, W), BF16)],
        [coords, plane] + [moved(plane, ("z",), k) for k in (1, 2, 3)],
        scratch=[pltpu.VMEM((W, 7 * E), F32)],
        limit=12,
        name="cube",
    )

    w_half = across(w_mine)

    ev = swapped(events[0])
    place = jnp.stack([y, lax.axis_index("xh")]).astype(I32)[None]
    line = jnp.pad(jnp.concatenate([place, lengths], axis=1), ((0, 0), (0, T - 6)))
    ints = swapped(jnp.concatenate([target_rows, position_ids, labels, line], axis=0))
    meta = ints
    (n0,) = call(norm_kernel, [sds((R, W), BF16)], [ev, line], n_smem=0, n_any=1, limit=12, name="norm")
    na = turned(n0, 1)
    nb = turned(n0, 3)
    na = tie(na, plane)
    nc = turned(na, 1)
    n0, nb, na = tie(n0, wg), tie(nb, wg), tie(na, nc)
    parts = [n0, na, nb, nc]
    parts = parts + [across(p) for p in parts]
    up = swapped(upstream[0])

    qkv = [sds((4, R, E), BF16), sds((8, R, E), BF16), sds((8, R, E), BF16)]
    a0, a1, a2, a3, q_s, k_s, v_s = call(
        forward_kernel, [sds((R + 16, E), BF16)] * 4 + qkv, [meta] + parts + [wg], flops=5 * 10**9,
        scratch=[pltpu.VMEM((4, R + 16, E), BF16)], name="forward",
    )
    r1, r2, r3 = ring(a1, 1), ring(a2, 2), ring(a3, 3)
    u, su, w_o, ev_t, emb, bpre, obs = call(
        side_kernel,
        [sds((R, W), BF16)] * 3 + [sds((T, W), F32)] + [sds((T, E), F32)] * 3,
        [meta, n0, w_mine, w_half, ev, ints, table, bias_w1, bias_w2.reshape(1, E)],
        flops=10**9,
        name="side",
    )

    def slopes(width, blocks, after):
        return call(
            slopes_kernel,
            [sds((4, R, width), BF16), sds((4, W, R), BF16), sds((4, E, R), BF16)],
            [meta] + blocks + [wg, after],
            n_any=1,
            flops=10**9,
            name="slopes",
        )

    s_a, nt_a, kt_a = slopes(3 * E, parts[:4], a0)
    w2 = head_w2.reshape(1, 2 * E)
    b2 = bias_w2.reshape(1, E)
    d0, d1, d2, d3, gated, d_out, dpre, picked, d_hid, active, d_rel, d_obs = call(
        middle_kernel,
        [sds((R, E), BF16)] * 4
        + [sds((R, W), BF16)] * 3
        + [sds((T, W), BF16), sds((T, 2 * E), BF16), sds((T, 2 * E), F32), sds((T, E), F32), sds((T, E), F32)],
        [meta, a0, r1, r2, r3, u, su, w_o, ev_t, obs, ints, up, head_w1, w2],
        scratch=[pltpu.VMEM((R, W), F32)],
        flops=10**9,
        name="middle",
    )
    g1, g2, g3 = ring(d1, 1), ring(d2, 2), ring(d3, 3)
    s_b, nt_b, kt_b = slopes(2 * E, parts[4:], d0)
    early, early_oth, s_own, s_oth = call(
        grads_kernel,
        [sds((R, 5 * E), BF16)] * 2 + [sds((R, E), BF16)] * 2,
        [meta, n0, dpre, gated, d_out, picked, d_hid, active, d_rel, d_obs, ints, emb, bpre, bias_w1, b2],
        flops=2 * 10**9,
        name="grads",
    )
    early_in = across(early_oth)
    late, late_oth = call(
        backward_kernel,
        [sds((R, 2 * E), BF16)] * 2,
        [meta, q_s, k_s, v_s, d0, g1, g2, g3, s_a, s_b, nt_a, nt_b, kt_a, kt_b, s_own, s_oth],
        scratch=[pltpu.VMEM((4, R, E), F32), pltpu.VMEM((8, R, E), F32), pltpu.VMEM((8, R, E), F32)]
        + [pltpu.VMEM((8, E, R), BF16), pltpu.VMEM((4, R, E), BF16)],
        flops=10**10,
        limit=28,
        name="backward",
    )
    late_in = across(late_oth)
    pair = jnp.concatenate(
        [
            (early.astype(F32) + early_in.astype(F32)).astype(BF16),
            (late.astype(F32) + late_in.astype(F32)).astype(BF16),
        ],
        axis=1,
    )
    got = lax.all_to_all(pair, CHIPS, 0, 0, tiled=True)
    g_in, g_out, g_h1, g_h2, g_tab, g_b1, g_b2 = call(
        sum_kernel,
        [sds((4, 4 * W), F32), sds((4, W), F32), sds((4, 2 * E), F32)]
        + [sds((1, 2), F32), sds((2, E), F32), sds((1, E), F32), sds((1, 1), F32)],
        [got],
        n_smem=0,
        name="total",
    )
    return g_in, g_out, g_h1, g_h2.reshape(2), g_tab, g_b1, g_b2.reshape(1)


def solution(mesh):
    fine = Mesh(mesh.devices.reshape(4, 2, 2, 4, 2), ("y", "xh", "xl", "z", "core"))
    ctx, dp = ("y", "xh"), ("xl", "z", "core")
    every = ctx + dp
    in_specs = (
        P(dp, ctx, None),
        P(dp, None),
        P(dp, ctx),
        P(dp, ctx),
        P(dp, ctx),
        P(dp, ctx, None),
        P(every, None),
        P(every, None),
        P(),
        P(),
        P(),
        P(),
        P(),
    )
    out_specs = (
        P(every, None),
        P(every, None),
        P(every, None),
        P(every),
        P(every, None),
        P(every, None),
        P(every),
    )
    return jax.shard_map(body, mesh=fine, in_specs=in_specs, out_specs=out_specs, check_vma=False)
```

```python
import functools
import math

import jax
import jax.numpy as jnp
from jax import lax
from jax.experimental import pallas as pl
from jax.experimental.pallas import tpu as pltpu
from jax.sharding import Mesh, PartitionSpec as P

HEADS = 4
EPSILON = 1e-05
HIGHEST = lax.Precision.HIGHEST
F32 = jnp.float32
BF16 = jnp.bfloat16
I32 = jnp.int32
R = 512
W = 512
E = 128
T = 128
SCALE = 1.0 / math.sqrt(E)
HALF = 0.5 * SCALE

NN = (((1,), (0,)), ((), ()))
NT = (((1,), (1,)), ((), ()))
TN = (((0,), (0,)), ((), ()))


def mm(a, b, dims=NN, precision=None):
    return lax.dot_general(a, b, dims, precision=precision, preferred_element_type=F32)


def silu_parts(z):
    h = 0.5 * z
    t = jnp.tanh(h)
    a = 1.0 + t
    w = h * a
    return w, 0.5 * (a + w * (1.0 - t))


def silu(z):
    h = 0.5 * z
    return h + h * jnp.tanh(h)


def vmem(n):
    return [pl.BlockSpec(memory_space=pltpu.VMEM)] * n


def smem():
    return [pl.BlockSpec(memory_space=pltpu.SMEM)]


def call(kernel, outs, args, scratch=(), limit=24, flops=0, n_smem=1, n_any=0, name=None):
    total = sum(a.size * a.dtype.itemsize for a in args) + sum(
        math.prod(o.shape) * o.dtype.itemsize for o in outs
    )
    return pl.pallas_call(
        kernel,
        out_shape=tuple(outs),
        in_specs=smem() * n_smem
        + vmem(len(args) - n_smem - n_any)
        + [pl.BlockSpec(memory_space=pl.ANY)] * n_any,
        out_specs=tuple(vmem(len(outs))),
        scratch_shapes=list(scratch),
        compiler_params=pltpu.CompilerParams(vmem_limit_bytes=limit << 20),
        cost_estimate=pl.CostEstimate(flops=flops, bytes_accessed=total, transcendentals=0),
        name=name,
    )(*args)


def sds(shape, dtype):
    return jax.ShapeDtypeStruct(shape, dtype)


def plane_kernel(coords, q0, q1, q2, q3, out):
    for k, ref in enumerate((q0, q1, q2, q3)):
        out[pl.ds(pl.multiple_of(((coords[1] + 4 - k) & 3) * 32, 32), 32), :] = ref[...]


def cube_kernel(coords, q0, q1, q2, q3, out, half, rows):
    for k, ref in enumerate((q0, q1, q2, q3)):
        z = ((coords[2] + 4 - k) & 3) * 8
        part = ref[...].astype(F32)
        for i in range(4):
            for j in range(4):
                at = i * 32 + j * 8
                rows[pl.ds(pl.multiple_of(j * E + i * 32 + z, 8), 8), :] = part[at : at + 8]
    out[...] = rows[:, : 3 * E].astype(BF16)
    half[...] = rows[:, 3 * E :].astype(BF16)


def norm_kernel(x_ref, _, o_ref):
    x = x_ref[...].astype(F32)
    mean = jnp.mean(x, axis=-1, keepdims=True)
    cen = x - mean
    inv = lax.rsqrt(jnp.mean(cen * cen, axis=-1, keepdims=True) + EPSILON)
    o_ref[...] = (cen * inv).astype(BF16)


def user_start(pos, meta):
    start = jnp.zeros_like(pos)
    end = 0
    for j in range(3):
        end = end + meta[3, 2 + j]
        start = jnp.where(pos >= end, end, start)
    return start


def places(y, core):
    s = jnp.where(core == 0, 3, 1)
    back, on, far = (y + s) & 3, (y + 4 - s) & 3, (y + 2) & 3
    return (y, back, on, far), (y, on, back, far)


def key_range(base, rows, meta):
    lo = user_start(base, meta)
    last = base + rows - 1
    end = last // R + 1
    first = lo // R
    diag = base // R
    full = jnp.clip((user_start(last, meta) + R - 1) // R, first, diag)
    return first, full, diag, end


def forward_kernel(meta, n0, na, nb, nc, o0, oa, ob, oc, wg, a0, a1, a2, a3, q_s, k_s, v_s, sent):
    y, core = meta[3, 0], meta[3, 1]
    own, oth = places(y, core)
    for blk, ref in zip(own, (n0, na, nb, nc)):
        b = 2 * blk + core
        p = silu(mm(ref[...], wg[:, : 3 * E])).astype(BF16)
        q_s[blk] = p[:, :E]
        k_s[b] = p[:, E : 2 * E]
        v_s[b] = p[:, 2 * E :]
    for blk, ref in zip(oth, (o0, oa, ob, oc)):
        b = 2 * blk + 1 - core
        p = silu(mm(ref[...], wg[:, E : 3 * E])).astype(BF16)
        k_s[b] = p[:, :E]
        v_s[b] = p[:, E:]
    rows = lax.broadcasted_iota(I32, (R, 1), 0)
    lanes = lax.broadcasted_iota(I32, (1, R), 1)

    def block(k, _):
        blk = (y + k) & 3
        c = 2 * blk + core
        q = q_s[blk]
        pos = rows + c * R
        start = user_start(pos, meta)

        def step(b, acc, masked):
            h = mm(q, k_s[b], NT) * HALF
            w = h + h * jnp.tanh(h)
            if masked:
                key_pos = lanes + b * R
                w = jnp.where((key_pos >= start) & (key_pos <= pos), w, 0.0)
            return acc + mm(w.astype(BF16), v_s[b])

        first, full, diag, end = key_range(c * R, R, meta)
        acc = jnp.zeros((R, E), F32)
        acc = lax.fori_loop(first, full, functools.partial(step, masked=True), acc)
        acc = lax.fori_loop(full, diag, functools.partial(step, masked=False), acc)
        acc = lax.fori_loop(diag, end, functools.partial(step, masked=True), acc)
        mean = jnp.mean(acc, axis=-1, keepdims=True).astype(BF16)
        sent[k, :R] = (acc - mean.astype(F32)).astype(BF16)
        one = (lax.broadcasted_iota(I32, (16, E), 1) == 0).astype(BF16)
        line = mm(one, jnp.broadcast_to(mean, (R, E)), NT)
        sent[k, R:] = jnp.concatenate(
            [line[0:1, i * E : (i + 1) * E] for i in range(4)] + [jnp.zeros((12, E), F32)], axis=0
        ).astype(BF16)
        return 0

    lax.fori_loop(0, 4, block, 0)
    for k, out in enumerate((a0, a1, a2, a3)):
        out[...] = sent[k]


def side_kernel(
    meta, n0, w_mine, wo_half, events, ints, table, bias_w1, bias_w2, u, su, w_out, ev_t, emb, bpre, obs
):
    first = meta[3, 1] == 0
    mine = w_mine[...]
    other = wo_half[...]
    w_u = jnp.where(first, mine, other)
    w_out[...] = jnp.where(first, other, mine)
    act, slope = silu_parts(mm(n0[...], w_u))
    u[...] = act.astype(BF16)
    su[...] = slope.astype(BF16)
    placing = (lax.broadcasted_iota(I32, (R, T), 0) == ints[0:1, :]).astype(BF16)
    ev_t[...] = mm(placing, events[...], TN)
    pid = jnp.broadcast_to(ints[1:2, :], (T, T)).astype(F32).T.astype(I32)
    pid = jnp.concatenate([pid, pid], axis=1)
    selector = (lax.broadcasted_iota(I32, (T, 2 * T), 1) == pid).astype(F32)
    embedded = mm(selector, table[...], precision=HIGHEST)
    bias_pre = mm(embedded, bias_w1[...], precision=HIGHEST)
    emb[...] = embedded
    bpre[...] = bias_pre
    hid = silu(bias_pre)
    obs[...] = jnp.broadcast_to(jnp.sum(hid * bias_w2[...], axis=1, keepdims=True), (T, E))


def slopes_kernel(meta, n0, na, nb, nc, wg, _, s_o, nt, kt):
    y, core = meta[3, 0], meta[3, 1]
    width = s_o.shape[2]
    own, oth = places(y, core)
    for blk, ref in zip(own if width == 3 * E else oth, (n0, na, nb, nc)):
        x = ref[...]
        act, slope = silu_parts(mm(x, wg[:, 3 * E - width : 3 * E]))
        s_o[blk] = slope.astype(BF16)
        kt[blk] = act[:, width - 2 * E : width - E].astype(BF16).T
        nt[blk] = x.T


def middle_kernel(
    meta, r0, r1, r2, r3, u, su, w_out, ev_t, obs, ints, upstream, head_w1, head_w2,
    d0, d1, d2, d3, gated_o, dout_o, dpre_o, picked_o, dhid_o, act_o, drel_o, dobs_o,
    att,
):
    y = meta[3, 0]
    for k, ref in enumerate((r0, r1, r2, r3)):
        h = (y + 4 - k) & 3
        means = ref[R:]
        pick = lax.broadcasted_iota(I32, (16, E), 0)
        column = jnp.concatenate([mm(means, (pick == i).astype(BF16), TN) for i in range(4)], axis=0)
        att[:, pl.ds(pl.multiple_of(h * E, E), E)] = ref[:R].astype(F32) + column
    x = att[...]
    mean = jnp.mean(x, axis=-1, keepdims=True)
    cen = x - mean
    inv = lax.rsqrt(jnp.mean(cen * cen, axis=-1, keepdims=True) + EPSILON)
    normed = cen * inv
    gate = u[...].astype(F32)
    gated = (normed * gate).astype(BF16)
    gated_o[...] = gated
    placing = (lax.broadcasted_iota(I32, (R, T), 0) == ints[0:1, :]).astype(BF16)
    gated_t = mm(placing, gated, TN).astype(BF16)
    picked = (mm(gated_t, w_out[...]) + ev_t[...]).astype(BF16)
    picked_o[...] = picked
    hidden = mm(picked, head_w1[...])
    active, slope = silu_parts(hidden)
    act_o[...] = active
    w2 = head_w2[...]
    relevance = jnp.sum(active * w2, axis=1, keepdims=True)
    observe = obs[:, :1]
    clicked = jnp.broadcast_to(ints[2:3, :], (T, T)).astype(F32).T[:, :1]
    rel_sig = jax.nn.sigmoid(relevance)
    obs_sig = jax.nn.sigmoid(observe)
    missing = jax.nn.sigmoid(-relevance) + rel_sig * jax.nn.sigmoid(-observe)
    d_rel = clicked * (rel_sig - 1.0) + (1.0 - clicked) * rel_sig * (1.0 - rel_sig) * obs_sig / missing
    d_obs = clicked * (obs_sig - 1.0) + (1.0 - clicked) * rel_sig * obs_sig * (1.0 - obs_sig) / missing
    drel_o[...] = jnp.broadcast_to(d_rel, (T, E))
    dobs_o[...] = jnp.broadcast_to(d_obs, (T, E))
    d_hidden = (d_rel * w2 * slope).astype(BF16)
    dhid_o[...] = d_hidden
    d_picked = mm(d_hidden, head_w1[...], NT).astype(BF16)
    d_out = (upstream[...].astype(F32) + mm(placing, d_picked)).astype(BF16)
    dout_o[...] = d_out
    d_gated = mm(d_out, w_out[...], NT)
    dpre_o[...] = (d_gated * normed * su[...].astype(F32)).astype(BF16)
    g = d_gated * gate
    first = jnp.mean(g, axis=-1, keepdims=True)
    second = jnp.mean(g * normed, axis=-1, keepdims=True)
    att[...] = inv * (g - first - normed * second)
    for k, ref in enumerate((d0, d1, d2, d3)):
        h = (y + k) & 3
        ref[...] = att[:, pl.ds(pl.multiple_of(h * E, E), E)].astype(BF16)


def packed(left, right):
    low = (lax.broadcasted_iota(I32, left.shape, 0) & 7) < 4
    n = left.shape[0]
    return jnp.where(low, left, pltpu.roll(right, 4, 0)), jnp.where(low, pltpu.roll(left, n - 4, 0), right)


def grads_kernel(
    meta, n0, dpre, gated, d_out, picked, d_hid, active, d_rel, d_obs, ints, emb, bpre, bias_w1, bias_w2,
    x_own, x_oth, s_own, s_oth,
):
    first = meta[3, 1] == 0

    def put(own_ref, oth_ref, col, left, right):
        x_0, x_1 = packed(left, right)
        cols = slice(col, col + left.shape[1])
        own_ref[:, cols] = jnp.where(first, x_0, x_1).astype(BF16)
        oth_ref[:, cols] = jnp.where(first, x_1, x_0).astype(BF16)

    g_u = mm(n0[...], dpre[...], TN)
    put(x_own, x_oth, 0, g_u[:, :256], g_u[:, 256:])
    g_wo = mm(gated[...], d_out[...], TN)
    put(x_own, x_oth, 256, g_wo[:, :256], g_wo[:, 256:])
    g_h1 = mm(picked[...], d_hid[...], TN)
    put(x_own, x_oth, 512, g_h1[:, :128], g_h1[:, 128:])
    hid, slope = silu_parts(bpre[...])
    d_bias = d_obs[...] * bias_w2[...] * slope
    g_b1 = mm(emb[...], d_bias, TN, HIGHEST)
    d_emb = mm(d_bias, bias_w1[...], NT, HIGHEST)
    pid = jnp.broadcast_to(ints[1:2, :], (2 * T, T))
    select_t = (lax.broadcasted_iota(I32, (2 * T, T), 0) == pid).astype(F32)
    g_tab = mm(select_t, d_emb, precision=HIGHEST)
    h2 = mm(active[...], d_rel[...], TN, HIGHEST)
    b2 = mm(hid, d_obs[...], TN, HIGHEST)
    lane2 = lax.broadcasted_iota(I32, (2 * T, E), 1)
    row2 = lax.broadcasted_iota(I32, (2 * T, E), 0)
    h2 = jnp.where(lane2 == (row2 & 1), h2, 0.0)
    b2 = jnp.where(lax.broadcasted_iota(I32, (T, E), 1) == 2, b2, 0.0)
    o2 = lax.broadcasted_iota(I32, (R, 2 * T), 0)
    i2 = lax.broadcasted_iota(I32, (R, 2 * T), 1)
    o1 = lax.broadcasted_iota(I32, (R, T), 0)
    i1 = lax.broadcasted_iota(I32, (R, T), 1)
    parts = []
    for cc in range(2):
        dest2 = 2 * (o2 >> 3) + cc
        dest1 = 2 * (o1 >> 3) + cc
        p_tab = (((o2 & 7) == 4) & (i2 == 2 * dest2)) | (((o2 & 7) == 5) & (i2 == 2 * dest2 + 1))
        p_h2 = ((o2 & 7) == 7) & ((i2 >> 1) == dest2)
        p_b1 = ((o1 & 7) == 6) & (i1 == dest1)
        p_b2 = ((o1 & 7) == 7) & (i1 == dest1)
        parts.append(
            mm(p_tab.astype(BF16), g_tab.astype(BF16))
            + mm(p_h2.astype(BF16), h2.astype(BF16))
            + mm(p_b1.astype(BF16), g_b1.astype(BF16))
            + mm(p_b2.astype(BF16), b2.astype(BF16))
        )
    s_own[...] = jnp.where(first, parts[0], parts[1]).astype(BF16)
    s_oth[...] = jnp.where(first, parts[1], parts[0]).astype(BF16)


def backward_kernel(
    meta, q_s, k_s, v_s, r0, r1, r2, r3, s_a, s_b, nt_a, nt_b, kt_a, kt_b, s_own, s_oth,
    x_own, x_oth,
    dq_s, dk_s, dv_s, kt_s, g_s,
):
    y, core = meta[3, 0], meta[3, 1]
    for i in range(4):
        kt_s[2 * i + core] = kt_a[i]
        kt_s[2 * i + 1 - core] = kt_b[i]
    dk_s[...] = jnp.zeros_like(dk_s)
    dv_s[...] = jnp.zeros_like(dv_s)
    rows = lax.broadcasted_iota(I32, (R, 1), 0)
    lanes = lax.broadcasted_iota(I32, (1, R), 1)
    for k, ref in enumerate((r0, r1, r2, r3)):
        g_s[(y + 4 - k) & 3] = ref[...]

    def block(blk, _):
        c = 2 * blk + core
        q = q_s[blk]
        g = g_s[blk]
        pos = lanes + c * R
        start = user_start(pos, meta)

        def step(b, dq, masked):
            kb = k_s[b]
            h = mm(kb, q, NT) * HALF
            dp = mm(v_s[b], g, NT)
            t = jnp.tanh(h)
            a = 1.0 + t
            w = h * a
            d = dp * (a + w * (1.0 - t))
            if masked:
                key_pos = rows + b * R
                keep = (key_pos >= start) & (key_pos <= pos)
                w = jnp.where(keep, w, 0.0)
                d = jnp.where(keep, d, 0.0)
            w = w.astype(BF16)
            d = d.astype(BF16)
            dv_s[b] += mm(w, g)
            dk_s[b] += mm(d, q)
            return dq + mm(kt_s[b], d)

        first, full, diag, end = key_range(c * R, R, meta)
        acc = jnp.zeros((E, R), F32)
        acc = lax.fori_loop(first, full, functools.partial(step, masked=True), acc)
        acc = lax.fori_loop(full, diag, functools.partial(step, masked=False), acc)
        acc = lax.fori_loop(diag, end, functools.partial(step, masked=True), acc)
        dq_s[blk] = acc.T
        return 0

    lax.fori_loop(0, 4, block, 0)
    g_all = jnp.zeros((W, 3 * E), F32)
    g_kv = jnp.zeros((W, 2 * E), F32)
    for i in range(4):
        b = 2 * i + core
        d = jnp.concatenate([dq_s[i] * HALF, dk_s[b] * HALF, dv_s[b]], axis=1) * s_a[i].astype(F32)
        g_all = g_all + mm(nt_a[i], d.astype(BF16))
        b = 2 * i + 1 - core
        d = jnp.concatenate([dk_s[b] * HALF, dv_s[b]], axis=1) * s_b[i].astype(F32)
        g_kv = g_kv + mm(nt_b[i], d.astype(BF16))
    g_q = g_all[:, :E]
    g_k = g_all[:, E : 2 * E] + g_kv[:, :E]
    g_v = g_all[:, 2 * E :] + g_kv[:, E:]
    first = core == 0
    low = (lax.broadcasted_iota(I32, (W, E), 0) & 7) < 4
    x_0, x_1 = packed(g_q, g_k)
    x_own[:, :E] = jnp.where(first, x_0, x_1).astype(BF16)
    x_oth[:, :E] = jnp.where(first, x_1, x_0).astype(BF16)
    v_1 = pltpu.roll(g_v, W - 4, 0)
    x_own[:, E:] = jnp.where(low, jnp.where(first, g_v, v_1), s_own[...].astype(F32)).astype(BF16)
    x_oth[:, E:] = jnp.where(low, jnp.where(first, v_1, g_v), s_oth[...].astype(F32)).astype(BF16)


def sum_kernel(x_ref, g_in, g_out, g_h1, g_h2, g_tab, g_b1, g_b2):
    total = None
    for h in range(HEADS):
        part = jnp.zeros((8, 7 * E), F32)
        for i in range(16):
            at = (h * 16 + i) * 8
            part = part + x_ref[at : at + 8, :].astype(F32)
        g_in[:, W + h * E : W + (h + 1) * E] = part[0:4, 6 * E :]
        g_in[:, 2 * W + h * E : 2 * W + (h + 1) * E] = part[0:4, 5 * E : 6 * E]
        g_in[:, 3 * W + h * E : 3 * W + (h + 1) * E] = part[4:8, 5 * E : 6 * E]
        total = part if total is None else total + part
    g_in[:, 0:256] = total[0:4, 0:256]
    g_in[:, 256:512] = total[4:8, 0:256]
    g_out[:, 0:256] = total[0:4, 256:512]
    g_out[:, 256:512] = total[4:8, 256:512]
    g_h1[:, 0:128] = total[0:4, 512:640]
    g_h1[:, 128:256] = total[4:8, 512:640]
    g_tab[...] = total[4:6, 768:896]
    g_b1[...] = total[6:7, 768:896]
    g_h2[...] = total[7:8, 768:770]
    g_b2[...] = total[7:8, 770:771]


CHIPS = ("y", "xh", "xl", "z")
SWAP = []
for _i in range(32):
    _xh, _rest, _core = _i // 16, (_i // 2) % 8, _i % 2
    SWAP.append((_i, _i if _xh == _core else (1 - _xh) * 16 + _rest * 2 + 1 - _core))


def swapped(x):
    return lax.ppermute(x, ("xh", "xl", "z", "core"), SWAP)


def across(x):
    return lax.ppermute(x, "core", [(0, 1), (1, 0)])


def ring(x, k):
    return lax.ppermute(x, "y", [(i, (i + k) % 4) for i in range(4)])


def moved(x, axes, k):
    return lax.ppermute(x, axes, [(i, (i + k) % 4) for i in range(4)])


def tie(x, other):
    space = pl.BlockSpec(memory_space=pltpu.VMEM)
    return pl.pallas_call(
        lambda *_: None,
        out_shape=sds(x.shape, x.dtype),
        in_specs=[space] * 2,
        out_specs=space,
        compiler_params=pltpu.CompilerParams(vmem_limit_bytes=4 << 20),
        input_output_aliases={0: 0},
        name="tie",
    )(x, other)


def turned(x, k):
    return lax.ppermute(
        x, ("y", "core"), [(2 * i + c, 2 * ((i + (k if c == 0 else -k)) % 4) + c) for i in range(4) for c in range(2)]
    )


def body(
    events, lengths, target_rows, position_ids, labels, upstream,
    w_in, w_out, head_w1, head_w2, table, bias_w1, bias_w2,
):
    y, core = lax.axis_index("y"), lax.axis_index("core")
    w_rows = jnp.concatenate([w_in, w_out], axis=1)
    w_other = across(w_rows)
    w_rows = jnp.where(
        core == 0, jnp.concatenate([w_rows, w_other], axis=0), jnp.concatenate([w_other, w_rows], axis=0)
    )
    shared = jnp.where(core == 0, w_rows[:, :W], w_rows[:, 4 * W :])
    w_rows = jnp.concatenate([w_rows[:, W : 4 * W], shared], axis=1)
    x, z = 2 * lax.axis_index("xh") + lax.axis_index("xl"), lax.axis_index("z")
    line = [moved(w_rows, ("y",), k) for k in (3, 2, 1)]
    line = jnp.concatenate(line + [w_rows] + line, axis=0)
    line = lax.dynamic_slice_in_dim(line, ((3 - y) & 3) * 8, 32, 0)
    line = jnp.concatenate(
        [lax.dynamic_slice_in_dim(line, at + y * E, E, 1) for at in (W, 2 * W, 0)] + [line[:, 3 * W :]], axis=1
    )
    lens = jnp.where(core == lax.axis_index("xh"), lengths, across(lengths))
    coords = jnp.concatenate([jnp.stack([y, x, z]).astype(I32), lens[0], core.astype(I32)[None]])
    early_meta = jnp.concatenate([coords[0:1], coords[7:8], coords[3:7]])[None]
    early_meta = jnp.broadcast_to(early_meta, (4, 6))
    (plane,) = call(
        plane_kernel,
        [sds((E, 7 * E), BF16)],
        [coords, line] + [moved(line, ("xh", "xl"), k) for k in (1, 2, 3)],
        limit=8,
        name="plane",
    )
    wg, w_mine = call(
        cube_kernel,
        [sds((W, 3 * E), BF16), sds((W, W), BF16)],
        [coords, plane] + [moved(plane, ("z",), k) for k in (1, 2, 3)],
        scratch=[pltpu.VMEM((W, 7 * E), F32)],
        limit=12,
        name="cube",
    )

    w_half = across(w_mine)

    ev = swapped(events[0])
    place = jnp.stack([y, lax.axis_index("xh")]).astype(I32)[None]
    line = jnp.pad(jnp.concatenate([place, lengths], axis=1), ((0, 0), (0, T - 6)))
    ints = swapped(jnp.concatenate([target_rows, position_ids, labels, line], axis=0))
    meta = ints
    (n0,) = call(norm_kernel, [sds((R, W), BF16)], [ev, line], n_smem=0, n_any=1, limit=12, name="norm")
    na = turned(n0, 1)
    nb = turned(n0, 3)
    na = tie(na, plane)
    nc = turned(na, 1)
    n0, nb, na = tie(n0, wg), tie(nb, wg), tie(na, nc)
    parts = [n0, na, nb, nc]
    parts = parts + [across(p) for p in parts]
    up = swapped(upstream[0])

    qkv = [sds((4, R, E), BF16), sds((8, R, E), BF16), sds((8, R, E), BF16)]
    a0, a1, a2, a3, q_s, k_s, v_s = call(
        forward_kernel, [sds((R + 16, E), BF16)] * 4 + qkv, [early_meta] + parts + [wg], flops=5 * 10**9,
        scratch=[pltpu.VMEM((4, R + 16, E), BF16)], name="forward",
    )
    r1, r2, r3 = ring(a1, 1), ring(a2, 2), ring(a3, 3)
    u, su, w_o, ev_t, emb, bpre, obs = call(
        side_kernel,
        [sds((R, W), BF16)] * 3 + [sds((T, W), F32)] + [sds((T, E), F32)] * 3,
        [meta, n0, w_mine, w_half, ev, ints, table, bias_w1, bias_w2.reshape(1, E)],
        flops=10**9,
        name="side",
    )

    def slopes(width, blocks, after):
        return call(
            slopes_kernel,
            [sds((4, R, width), BF16), sds((4, W, R), BF16), sds((4, E, R), BF16)],
            [meta] + blocks + [wg, after],
            n_any=1,
            flops=10**9,
            name="slopes",
        )

    s_a, nt_a, kt_a = slopes(3 * E, parts[:4], a0)
    w2 = head_w2.reshape(1, 2 * E)
    b2 = bias_w2.reshape(1, E)
    d0, d1, d2, d3, gated, d_out, dpre, picked, d_hid, active, d_rel, d_obs = call(
        middle_kernel,
        [sds((R, E), BF16)] * 4
        + [sds((R, W), BF16)] * 3
        + [sds((T, W), BF16), sds((T, 2 * E), BF16), sds((T, 2 * E), F32), sds((T, E), F32), sds((T, E), F32)],
        [meta, a0, r1, r2, r3, u, su, w_o, ev_t, obs, ints, up, head_w1, w2],
        scratch=[pltpu.VMEM((R, W), F32)],
        flops=10**9,
        name="middle",
    )
    g1, g2, g3 = ring(d1, 1), ring(d2, 2), ring(d3, 3)
    s_b, nt_b, kt_b = slopes(2 * E, parts[4:], d0)
    early, early_oth, s_own, s_oth = call(
        grads_kernel,
        [sds((R, 5 * E), BF16)] * 2 + [sds((R, E), BF16)] * 2,
        [meta, n0, dpre, gated, d_out, picked, d_hid, active, d_rel, d_obs, ints, emb, bpre, bias_w1, b2],
        flops=2 * 10**9,
        name="grads",
    )
    early_in = across(early_oth)
    late, late_oth = call(
        backward_kernel,
        [sds((R, 2 * E), BF16)] * 2,
        [meta, q_s, k_s, v_s, d0, g1, g2, g3, s_a, s_b, nt_a, nt_b, kt_a, kt_b, s_own, s_oth],
        scratch=[pltpu.VMEM((4, R, E), F32), pltpu.VMEM((8, R, E), F32), pltpu.VMEM((8, R, E), F32)]
        + [pltpu.VMEM((8, E, R), BF16), pltpu.VMEM((4, R, E), BF16)],
        flops=10**10,
        limit=28,
        name="backward",
    )
    late_in = across(late_oth)
    pair = jnp.concatenate(
        [
            (early.astype(F32) + early_in.astype(F32)).astype(BF16),
            (late.astype(F32) + late_in.astype(F32)).astype(BF16),
        ],
        axis=1,
    )
    got = lax.all_to_all(pair, CHIPS, 0, 0, tiled=True)
    g_in, g_out, g_h1, g_h2, g_tab, g_b1, g_b2 = call(
        sum_kernel,
        [sds((4, 4 * W), F32), sds((4, W), F32), sds((4, 2 * E), F32)]
        + [sds((1, 2), F32), sds((2, E), F32), sds((1, E), F32), sds((1, 1), F32)],
        [got],
        n_smem=0,
        name="total",
    )
    return g_in, g_out, g_h1, g_h2.reshape(2), g_tab, g_b1, g_b2.reshape(1)


def solution(mesh):
    fine = Mesh(mesh.devices.reshape(4, 2, 2, 4, 2), ("y", "xh", "xl", "z", "core"))
    ctx, dp = ("y", "xh"), ("xl", "z", "core")
    every = ctx + dp
    in_specs = (
        P(dp, ctx, None),
        P(dp, None),
        P(dp, ctx),
        P(dp, ctx),
        P(dp, ctx),
        P(dp, ctx, None),
        P(every, None),
        P(every, None),
        P(),
        P(),
        P(),
        P(),
        P(),
    )
    out_specs = (
        P(every, None),
        P(every, None),
        P(every, None),
        P(every),
        P(every, None),
        P(every, None),
        P(every),
    )
    return jax.shard_map(body, mesh=fine, in_specs=in_specs, out_specs=out_specs, check_vma=False)
```
